256 devices in a mesh: ctx: 64 (over x, z, y_lo), ts: 4 (over y_hi, core).
Axes of the slice: x: 4, y: 4 (y_hi: 2, y_lo: 2; y = y_hi * 2 + y_lo), z: 8, core: 2. Of those that a mesh axis runs over, the one named last changes fastest.
Arguments:
- se_input: bfloat16 [16384, 3, 4096], P('ctx', None, 'ts'), may hold values from -6 to 6
- mr_input: bfloat16 [16384, 2, 4096], P('ctx', None, 'ts'), may hold values from -6 to 6
- cotangent: bfloat16 [16384, 4096], P('ctx', 'ts'), may hold values from -6 to 6
- se_featurizer: float32 [3, 3, 4096], P(None, None, 'ts'), may hold values from -3.5 to 3.5
- mr_featurizer: float32 [3, 3, 4096], P(None, None, 'ts'), may hold values from -3.5 to 3.5
- se_filter: float32 [7, 4096], P(None, 'ts'), may hold values from -2 to 2
- mr_filter: float32 [128, 4096], P(None, 'ts'), may hold values from -1 to 1
- decay_rate: float32 [4096], P('ts'), may hold values from 0.003 to 0.05
Outputs:
- grad_se_input: bfloat16 [16384, 3, 4096], P('ctx', None, 'ts')
- grad_mr_input: bfloat16 [16384, 2, 4096], P('ctx', None, 'ts')
- grad_se_filter: float32 [7, 4096], P(None, 'ts')
- grad_mr_filter: float32 [128, 4096], P(None, 'ts')
The draws below stay inside these ranges and needn't reach their ends.
All inputs are finite; a program needn't handle non-finite values.
Results may differ from the reference program's by a relative error of at most 0.0061.
Values may be sent and summed in bfloat16 or wider, within the bound.
No kernel may reach another device: no remote copies, remote signals or barrier semaphores. Data moves between devices by JAX's collectives and lax.ppermute only.
A program may use at most 128 MiB of HBM per device.

```python
import math
import jax
import jax.numpy as jnp
from jax import lax

C = 4096
LF = 3
LS = 7
LM = 128
TOKENS = 16384


def block_levels(stream_key, extent, split, smallest, largest):
    def one(axis_at, blocks):
        steps = jax.random.uniform(jax.random.fold_in(jax.random.fold_in(stream_key, 6), axis_at), (blocks,), jnp.float32, smallest / len(split), largest / len(split))
        return jnp.repeat(jnp.exp(steps), extent[axis_at] // blocks).reshape((-1,) + (1,) * (len(extent) - axis_at - 1))

    gain = one(*split[0])
    for cut in split[1:]:
        gain = gain * one(*cut)
    return gain


def bell_draw(rng, dims, deviation, limit, cuts=(), kind=jnp.bfloat16):
    factor_of = block_levels(rng, dims, cuts, -0.22, 0.18) if cuts else 1.0
    values = jax.random.normal(rng, dims, jnp.float32) * deviation * factor_of
    return jnp.minimum(jnp.maximum(values, -limit), limit).astype(kind)


def setup_inputs(seed: int = 0) -> dict:
    keys = jax.random.split(jax.random.key(seed), 9)
    return {
        "se_input": bell_draw(keys[0], (TOKENS, 3, C), 1.0, 6.0, ((0, 64), (2, 4))),
        "mr_input": bell_draw(keys[1], (TOKENS, 2, C), 1.0, 6.0, ((0, 64), (2, 4))),
        "cotangent": bell_draw(keys[2], (TOKENS, C), 1.0, 6.0, ((0, 64), (1, 4))),
        "se_featurizer": bell_draw(keys[3], (LF, 3, C), LF ** -0.5, 3.5, ((2, 4),), jnp.float32),
        "mr_featurizer": bell_draw(keys[4], (LF, 3, C), LF ** -0.5, 3.5, ((2, 4),), jnp.float32),
        "se_filter": bell_draw(keys[5], (LS, C), LS ** -0.5, 2.0, ((1, 4),), jnp.float32),
        "mr_filter": bell_draw(keys[6], (LM, C), (LM // 4) ** -0.5, 1.0, ((1, 4),), jnp.float32),
        "decay_rate": jnp.clip(jnp.exp(math.log(0.05) - 2.8134107 * jax.random.uniform(keys[7], (C,), jnp.float32) ** block_levels(keys[7], (C,), ((0, 4),), -0.2, 0.2)), 0.003, 0.05),
    }


def causal_sum(signal, kernel):
    tap_count = kernel.shape[0]
    row_count = signal.shape[0]
    padded = jnp.pad(signal, ((tap_count - 1, 0), (0, 0)))
    summed = jnp.zeros_like(signal)
    for offset in range(tap_count):
        begin = tap_count - 1 - offset
        summed = summed + kernel[offset] * padded[begin:begin + row_count]
    return summed

def ahead_sum(signal, kernel):
    tap_count = kernel.shape[0]
    row_count = signal.shape[0]
    padded = jnp.pad(signal, ((0, tap_count - 1), (0, 0)))
    summed = jnp.zeros_like(signal)
    for offset in range(tap_count):
        summed = summed + kernel[offset] * padded[offset:offset + row_count]
    return summed

def lag_sums(upstream, history, tap_count):
    row_count = upstream.shape[0]
    padded = jnp.pad(history, ((tap_count - 1, 0), (0, 0)))
    pieces = []
    for offset in range(tap_count):
        begin = tap_count - 1 - offset
        pieces.append(lax.optimization_barrier(jnp.sum(upstream * padded[begin:begin + row_count], axis=0)))
    return jnp.stack(pieces, axis=0)

def reference(se_input, mr_input, cotangent, se_featurizer, mr_featurizer, se_filter, mr_filter, decay_rate):
    block_width = min(128, C)
    block_count = C // block_width
    norm_factor = 1.0 / math.sqrt(TOKENS)
    lag_steps = jnp.arange(LM, dtype=jnp.float32)[:, None]

    def columns(source, start):
        return lax.dynamic_slice_in_dim(source, start, block_width, axis=1)

    def part_columns(source, part, start):
        return lax.dynamic_slice_in_dim(source[:, part, :], start, block_width, axis=1)

    def one_block(block_index):
        start = (block_index * block_width).astype(jnp.int32)
        se_query_taps = part_columns(se_featurizer, 0, start)
        se_key_taps = part_columns(se_featurizer, 1, start)
        se_value_taps = part_columns(se_featurizer, 2, start)
        mr_query_taps = part_columns(mr_featurizer, 0, start)
        mr_key_taps = part_columns(mr_featurizer, 1, start)
        mr_value_taps = part_columns(mr_featurizer, 2, start)
        query_one = causal_sum(part_columns(se_input, 0, start).astype(jnp.float32), se_query_taps)
        key_one = causal_sum(part_columns(se_input, 1, start).astype(jnp.float32), se_key_taps)
        value_one = causal_sum(part_columns(se_input, 2, start).astype(jnp.float32), se_value_taps)
        product_one = (key_one * value_one).astype(jnp.bfloat16).astype(jnp.float32)
        short_kernel = columns(se_filter, start)
        mixed_one = causal_sum(product_one, short_kernel)
        output_one = (query_one * mixed_one).astype(jnp.bfloat16)
        query_two = causal_sum(part_columns(mr_input, 0, start).astype(jnp.float32), mr_query_taps)
        key_two = causal_sum(part_columns(mr_input, 1, start).astype(jnp.float32), mr_key_taps)
        value_two = causal_sum(output_one.astype(jnp.float32), mr_value_taps)
        product_two = (key_two * value_two).astype(jnp.bfloat16).astype(jnp.float32)
        rates = lax.dynamic_slice_in_dim(decay_rate, start, block_width)
        damping = jnp.exp(-lag_steps * rates[None, :])
        medium_kernel = columns(mr_filter, start) * damping
        mixed_two = causal_sum(product_two, medium_kernel)
        upstream = columns(cotangent, start).astype(jnp.float32)
        grad_query_two = upstream * mixed_two
        grad_mixed_two = upstream * query_two
        grad_product_two = ahead_sum(grad_mixed_two, medium_kernel)
        medium_grad = lag_sums(grad_mixed_two, product_two, LM) * damping * norm_factor
        grad_mr_query = ahead_sum(grad_query_two, mr_query_taps)
        grad_mr_key = ahead_sum(grad_product_two * value_two, mr_key_taps)
        grad_output_one = ahead_sum(grad_product_two * key_two, mr_value_taps)
        grad_query_one = grad_output_one * mixed_one
        grad_mixed_one = grad_output_one * query_one
        grad_product_one = ahead_sum(grad_mixed_one, short_kernel)
        short_grad = lag_sums(grad_mixed_one, product_one, LS) * norm_factor
        grad_se_query = ahead_sum(grad_query_one, se_query_taps)
        grad_se_key = ahead_sum(grad_product_one * value_one, se_key_taps)
        grad_se_value = ahead_sum(grad_product_one * key_one, se_value_taps)
        se_parts = jnp.stack([grad_se_query, grad_se_key, grad_se_value], axis=0).astype(jnp.bfloat16)
        mr_parts = jnp.stack([grad_mr_query, grad_mr_key], axis=0).astype(jnp.bfloat16)
        return (se_parts, mr_parts, short_grad, medium_grad)
    se_parts, mr_parts, short_grads, medium_grads = lax.map(one_block, jnp.arange(block_count, dtype=jnp.int32))
    grad_se_input = jnp.transpose(se_parts, (2, 1, 0, 3)).reshape(TOKENS, 3, C)
    grad_mr_input = jnp.transpose(mr_parts, (2, 1, 0, 3)).reshape(TOKENS, 2, C)
    grad_se_filter = jnp.transpose(short_grads, (1, 0, 2)).reshape(LS, C)
    grad_mr_filter = jnp.transpose(medium_grads, (1, 0, 2)).reshape(LM, C)
    return (grad_se_input, grad_mr_input, grad_se_filter, grad_mr_filter)
```

```python
import math

import jax
import jax.numpy as jnp
from jax import lax
from jax.sharding import PartitionSpec as P


def for_sending(shard):
    return jax.tree.map(lambda a: a.astype(jnp.bfloat16) if a.dtype == jnp.float32 else a, shard)


def from_behind(shard, axis, by):
    count = lax.axis_size(axis)
    pairs = [(i, i + by) for i in range(count) if 0 <= i + by < count]
    return lax.ppermute(shard, axis, pairs)


def depthwise(extended, kernel):
    result = lax.conv_general_dilated(
        extended[None],
        kernel[:, None, :],
        (1,),
        "VALID",
        dimension_numbers=("NWC", "WIO", "NWC"),
        feature_group_count=extended.shape[1],
        precision=lax.Precision.HIGHEST,
    )
    return result[0]


def causal_mix(extended, kernel):
    return depthwise(extended, kernel[::-1])


def reverse_mix(extended, kernel):
    return depthwise(extended, kernel)


def tap_sums(history, upstream):
    return depthwise(history, upstream)[::-1]


def before_ctx(source, rim_depth):
    return from_behind(for_sending(source[source.shape[0] - rim_depth :]), "ctx", 1)


def after_ctx(source, rim_depth):
    return from_behind(source[:rim_depth], "ctx", -1)


def operators(
    se_parts,
    mr_parts,
    cotangent,
    se_taps,
    mr_taps,
    short_kernel,
    medium_taps,
    decay_full,
    before,
    after,
):
    row_count = cotangent.shape[0]
    channels = cotangent.shape[1]
    feat_length = se_taps.shape[0]
    short_length = short_kernel.shape[0]
    medium_length = medium_taps.shape[0]
    se_input = se_parts.reshape(row_count, 3 * channels)
    mr_input = mr_parts.reshape(row_count, 2 * channels)
    se_featurizer = se_taps.reshape(feat_length, 3 * channels)
    mr_featurizer = mr_taps.reshape(feat_length, 3 * channels)
    lag_steps = jnp.arange(medium_length, dtype=jnp.float32)[:, None]
    damping = jnp.exp(-decay_full[None, :] * lag_steps)
    medium_kernel = medium_taps * damping
    extended = jnp.concatenate([before(se_input, feat_length - 1), se_input], axis=0)
    featured = causal_mix(extended.astype(jnp.float32), se_featurizer)
    se_product = (featured[:, channels : 2 * channels] * featured[:, 2 * channels :]).astype(
        jnp.bfloat16
    )
    se_history = jnp.concatenate([before(se_product, short_length - 1), se_product], axis=0)
    se_query = featured[:, :channels]
    se_key = featured[:, channels : 2 * channels]
    se_value = featured[:, 2 * channels :]
    se_history_wide = se_history.astype(jnp.float32)
    se_mixed = causal_mix(se_history_wide, short_kernel)
    se_output = (se_query * se_mixed).astype(jnp.bfloat16)
    mr_source = jnp.concatenate([mr_input, se_output], axis=1)
    mr_extended = jnp.concatenate([before(mr_source, feat_length - 1), mr_source], axis=0)
    mr_featured = causal_mix(mr_extended.astype(jnp.float32), mr_featurizer)
    mr_query = mr_featured[:, :channels]
    mr_key = mr_featured[:, channels : 2 * channels]
    mr_value = mr_featured[:, 2 * channels :]
    mr_product = (mr_key * mr_value).astype(jnp.bfloat16)
    mr_history = jnp.concatenate(
        [before(mr_product, medium_length - 1), mr_product], axis=0
    ).astype(jnp.float32)
    mr_mixed = causal_mix(mr_history, medium_kernel)
    upstream = cotangent.astype(jnp.float32)
    grad_query = upstream * mr_mixed
    grad_mixed = upstream * mr_query
    grad_product = reverse_mix(
        jnp.concatenate([grad_mixed, after(grad_mixed, medium_length - 1)], axis=0), medium_kernel
    )
    medium_grad = tap_sums(mr_history, grad_mixed) * damping
    mr_feature_grad = jnp.concatenate(
        [grad_query, grad_product * mr_value, grad_product * mr_key], axis=1
    )
    mr_back = reverse_mix(
        jnp.concatenate([mr_feature_grad, after(mr_feature_grad, feat_length - 1)], axis=0),
        mr_featurizer,
    )
    grad_mr_input = mr_back[:, : 2 * channels].astype(jnp.bfloat16).reshape(row_count, 2, channels)
    grad_se_output = mr_back[:, 2 * channels :]
    se_grad_query = grad_se_output * se_mixed
    se_grad_mixed = grad_se_output * se_query
    se_grad_product = reverse_mix(
        jnp.concatenate([se_grad_mixed, after(se_grad_mixed, short_length - 1)], axis=0),
        short_kernel,
    )
    short_grad = tap_sums(se_history_wide, se_grad_mixed)
    se_feature_grad = jnp.concatenate(
        [se_grad_query, se_grad_product * se_value, se_grad_product * se_key], axis=1
    )
    se_back = reverse_mix(
        jnp.concatenate([se_feature_grad, after(se_feature_grad, feat_length - 1)], axis=0),
        se_featurizer,
    )
    grad_se_input = se_back.astype(jnp.bfloat16).reshape(row_count, 3, channels)
    return (grad_se_input, grad_mr_input, short_grad, medium_grad)


def ctx_sums(short_part, medium_part):
    count = lax.axis_size("ctx")
    short_length, channels = short_part.shape
    medium_length = medium_part.shape[0]
    short_rows = jnp.pad(short_part, ((0, -short_length % 8), (0, 0)))
    depth = medium_length // count
    width = short_rows.size // (count * depth)
    terms = jnp.concatenate(
        [
            medium_part.astype(jnp.bfloat16).reshape(count, depth, channels),
            short_rows.astype(jnp.bfloat16).reshape(count, depth, width),
        ],
        axis=2,
    )
    shares = lax.all_to_all(terms, "ctx", 0, 0, tiled=True)
    total = jnp.sum(shares.astype(jnp.float32), axis=0).astype(jnp.bfloat16)
    copies = jnp.broadcast_to(total[None], (count,) + total.shape)
    totals = lax.all_to_all(copies, "ctx", 0, 0, tiled=True).astype(jnp.float32)
    medium_total = totals[:, :, :channels].reshape(medium_length, channels)
    short_total = totals[:, :, channels:].reshape(short_rows.shape)[:short_length]
    return short_total, medium_total


def local(
    se_input, mr_input, cotangent, se_featurizer, mr_featurizer, se_filter, mr_filter, decay_rate
):
    norm_factor = 1.0 / math.sqrt(cotangent.shape[0] * lax.axis_size("ctx"))
    grad_se_input, grad_mr_input, short_grad, medium_grad = operators(
        se_input,
        mr_input,
        cotangent,
        se_featurizer,
        mr_featurizer,
        se_filter,
        mr_filter,
        decay_rate,
        before_ctx,
        after_ctx,
    )
    short_total, medium_total = ctx_sums(short_grad * norm_factor, medium_grad * norm_factor)
    return (grad_se_input, grad_mr_input, short_total, medium_total)


def solution(mesh):
    placed = (
        P("ctx", None, "ts"),
        P("ctx", None, "ts"),
        P("ctx", "ts"),
        P(None, None, "ts"),
        P(None, None, "ts"),
        P(None, "ts"),
        P(None, "ts"),
        P("ts"),
    )
    return jax.shard_map(
        local,
        mesh=mesh,
        in_specs=placed,
        out_specs=(P("ctx", None, "ts"), P("ctx", None, "ts"), P(None, "ts"), P(None, "ts")),
        check_vma=False,
    )
```

```python
import functools
import math

import jax
import jax.numpy as jnp
import ml_dtypes
import numpy as np
from jax import lax
from jax.experimental import pallas as pl
from jax.experimental.pallas import tpu as pltpu
from jax.sharding import PartitionSpec as P

F32 = jnp.float32
BF16 = jnp.bfloat16
LANES = 128
BLOCK = 256
PAD = 16
REACH = 16
POINTS = 400
HALF = POINTS // 2
DEPTH = 512


def chunks(begin, end, step=32):
    return [(a, min(step, end - a)) for a in range(begin, end, step)]


def split(value):
    high = value.astype(BF16)
    return high, (value - high.astype(F32)).astype(BF16)


def transform_tables():
    frequency = (np.arange(HALF) + 0.5)[:, None]
    angle = 2.0 * np.pi * frequency * np.arange(POINTS)[None, :] / POINTS
    forward = np.concatenate([np.cos(angle), -np.sin(angle)], axis=0)
    back = forward.T
    lags = back[128 - np.arange(128)]
    tables = []
    for table in (forward, back, lags):
        table = np.pad(table, ((0, 0), (0, DEPTH - POINTS)))
        high = table.astype(ml_dtypes.bfloat16)
        low = (table - high.astype(np.float64)).astype(ml_dtypes.bfloat16)
        tables.append(np.stack([high, low]))
    return tables


def weighted(ref, lead, row, count, taps, step):
    total = ref[lead + (pl.ds(row, count), slice(None))] * taps[0]
    for j in range(1, len(taps)):
        total = total + ref[lead + (pl.ds(row + step * j, count), slice(None))] * taps[j]
    return total


def rounded(value):
    return value.astype(BF16).astype(F32)


def edge_kernel(
    se_ref, mr_ref, g_ref, sw_ref, mw_ref, sf_ref, on_ref, back_ref, x, q1, ps, y1, tail
):
    rows = se_ref.shape[1]
    first = rows - 144
    for h in range(BLOCK // LANES):
        lanes = slice(h * LANES, (h + 1) * LANES)
        sw = [[sw_ref[j, p, lanes][None, :] for j in range(3)] for p in range(3)]
        mw = [[mw_ref[j, p, lanes][None, :] for j in range(3)] for p in range(3)]
        sf = [sf_ref[j, lanes][None, :] for j in range(7)]
        for a, n in chunks(0, 144):
            for p in range(3):
                x[p, pl.ds(a, n), :] = se_ref[p, pl.ds(first + a, n), lanes].astype(F32)
            x[3, pl.ds(a, n), :] = mr_ref[1, pl.ds(first + a, n), lanes].astype(F32)
        for a, n in [(8, 8)] + chunks(16, 144):
            k1 = weighted(x, (1,), a, n, sw[1], -1)
            v1 = weighted(x, (2,), a, n, sw[2], -1)
            ps[pl.ds(a, n), :] = rounded(k1 * v1)
            q1[pl.ds(a, n), :] = weighted(x, (0,), a, n, sw[0], -1)
        for a, n in [(8, 8)] + chunks(16, 144):
            z1 = weighted(ps, (), a, n, sf, -1)
            y1[pl.ds(a, n), :] = rounded(q1[pl.ds(a, n), :] * z1)
        for a, n in chunks(16, 144):
            k2 = weighted(x, (3,), a, n, mw[1], -1)
            v2 = weighted(y1, (), a, n, mw[2], -1)
            on_ref[pl.ds(a - 16, n), lanes] = (k2 * v2).astype(BF16)
        tail[...] = jnp.zeros((32, LANES), F32)
        tail[0:6, :] = ps[138:144, :]
        tail[6:8, :] = y1[142:144, :]
        tail[8:10, :] = x[0, 142:144, :]
        tail[10:12, :] = x[1, 142:144, :]
        tail[12:14, :] = x[2, 142:144, :]
        tail[16:18, :] = x[3, 142:144, :]
        x[4, 0:16, :] = mr_ref[0, rows - 16 : rows, lanes].astype(F32)
        tail[14:16, :] = x[4, 14:16, :]
        on_ref[128:160, lanes] = tail[...].astype(BF16)

        x[3, 0:PAD, :] = jnp.zeros((PAD, LANES), F32)
        for a, n in chunks(0, 144):
            x[3, pl.ds(PAD + a, n), :] = mr_ref[0, pl.ds(a, n), lanes].astype(F32)
        for a, n in chunks(0, 144):
            q2 = weighted(x, (3,), PAD + a, n, mw[0], -1)
            back_ref[pl.ds(a, n), lanes] = (
                g_ref[pl.ds(a, n), lanes].astype(F32) * q2
            ).astype(BF16)
        x[0, 0:16, :] = se_ref[0, 0:16, lanes].astype(F32)
        x[1, 0:16, :] = se_ref[1, 0:16, lanes].astype(F32)
        x[2, 0:16, :] = se_ref[2, 0:16, lanes].astype(F32)
        x[4, 0:16, :] = mr_ref[1, 0:16, lanes].astype(F32)
        y1[0:16, :] = g_ref[0:16, lanes].astype(F32)
        tail[...] = jnp.zeros((32, LANES), F32)
        tail[0:2, :] = y1[0:2, :]
        tail[2:4, :] = x[3, PAD : PAD + 2, :]
        tail[4:14, :] = x[4, 0:10, :]
        tail[14:22, :] = x[0, 0:8, :]
        tail[22:24, :] = x[1, 0:2, :]
        tail[24:26, :] = x[2, 0:2, :]
        back_ref[144:176, lanes] = tail[...].astype(BF16)


def dot(a, b):
    return jnp.dot(a, b, preferred_element_type=F32)


def wide_dot(table, rows, columns, value):
    high, low = split(value)
    return (
        dot(table[0, rows, columns], high)
        + dot(table[1, rows, columns], high)
        + dot(table[0, rows, columns], low)
    )


def main_kernel(
    norm_factor,
    se_ref,
    mr_ref,
    g_ref,
    on_ref,
    back_ref,
    sw_ref,
    mw_ref,
    sf_ref,
    mf_ref,
    rate_ref,
    fwd_ref,
    inv_ref,
    lag_ref,
    se_out,
    mr_out,
    short_out,
    medium_out,
    x,
    gx,
    q1,
    k1,
    v1,
    ps,
    z1,
    y1,
    k2,
    v2,
    tail,
    pb,
    db,
    z2,
    w2,
    d,
    held,
):
    rows = se_ref.shape[1]
    end = rows + REACH
    halves = BLOCK // LANES
    top = lax.broadcasted_iota(jnp.int32, (REACH, LANES), 0) < 2

    def lanes_of(h):
        return slice(h * LANES, (h + 1) * LANES)

    for h in range(halves):
        lanes = lanes_of(h)
        sw = [[sw_ref[j, p, lanes][None, :] for j in range(3)] for p in range(3)]
        mw = [[mw_ref[j, p, lanes][None, :] for j in range(3)] for p in range(3)]
        sf = [sf_ref[j, lanes][None, :] for j in range(7)]
        for a, n in chunks(0, rows):
            for p in range(3):
                x[p, pl.ds(PAD + a, n), :] = se_ref[p, pl.ds(a, n), lanes].astype(F32)
            for p in range(2):
                x[3 + p, pl.ds(PAD + a, n), :] = mr_ref[p, pl.ds(a, n), lanes].astype(F32)
            gx[h, pl.ds(a, n), :] = g_ref[pl.ds(a, n), lanes].astype(F32)
        tail[...] = on_ref[128:160, lanes].astype(F32)
        ps[h, PAD - 6 : PAD, :] = tail[0:6, :]
        y1[PAD - 2 : PAD, :] = tail[6:8, :]
        for p in range(5):
            x[p, PAD - 2 : PAD, :] = tail[8 + 2 * p : 10 + 2 * p, :]
            x[p, PAD + rows : PAD + end, :] = jnp.zeros((REACH, LANES), F32)
        gx[h, rows:end, :] = jnp.zeros((REACH, LANES), F32)
        tail[...] = back_ref[144:176, lanes].astype(F32)
        gx[h, rows : rows + 2, :] = tail[0:2, :]
        x[3, PAD + rows : PAD + rows + 2, :] = tail[2:4, :]
        x[4, PAD + rows : PAD + rows + 10, :] = tail[4:14, :]
        x[0, PAD + rows : PAD + rows + 8, :] = tail[14:22, :]
        x[1, PAD + rows : PAD + rows + 2, :] = tail[22:24, :]
        x[2, PAD + rows : PAD + rows + 2, :] = tail[24:26, :]
        for t, n in chunks(0, end):
            r = PAD + t
            key = weighted(x, (1,), r, n, sw[1], -1)
            value = weighted(x, (2,), r, n, sw[2], -1)
            k1[h, pl.ds(t, n), :] = key
            v1[h, pl.ds(t, n), :] = value
            ps[h, pl.ds(r, n), :] = rounded(key * value)
            q1[h, pl.ds(t, n), :] = weighted(x, (0,), r, n, sw[0], -1)
        for t, n in chunks(0, end):
            r = PAD + t
            mixed = weighted(ps, (h,), r, n, sf, -1)
            z1[h, pl.ds(t, n), :] = mixed
            y1[pl.ds(r, n), :] = rounded(q1[h, pl.ds(t, n), :] * mixed)
        pb[0:128, lanes] = on_ref[0:128, lanes]
        for t, n in chunks(0, end):
            r = PAD + t
            key = weighted(x, (4,), r, n, mw[1], -1)
            value = weighted(y1, (), r, n, mw[2], -1)
            k2[h, pl.ds(t, n), :] = key
            v2[h, pl.ds(t, n), :] = value
            product = key * value
            upstream = gx[h, pl.ds(t, n), :] * weighted(x, (3,), r, n, mw[0], -1)
            if t == rows:
                product = jnp.where(top, product, 0.0)
                upstream = jnp.where(top, upstream, back_ref[0:REACH, lanes].astype(F32))
            pb[pl.ds(128 + t, n), lanes] = product.astype(BF16)
            high, low = split(upstream)
            db[0, pl.ds(t, n), lanes] = high
            db[1, pl.ds(t, n), lanes] = low
        db[0, end:POINTS, lanes] = back_ref[REACH : POINTS - rows, lanes]
        pb[POINTS:DEPTH, lanes] = jnp.zeros((DEPTH - POINTS, LANES), BF16)
        db[0, POINTS:DEPTH, lanes] = jnp.zeros((DEPTH - POINTS, LANES), BF16)

    whole = slice(None)
    lag = lax.broadcasted_iota(jnp.int32, (128, BLOCK), 0).astype(F32)
    damping = jnp.exp(-rate_ref[...] * lag)
    kernel = wide_dot(fwd_ref, whole, slice(0, 128), mf_ref[...] * damping * (2.0 / POINTS))
    product = dot(fwd_ref[0], pb[...]) + dot(fwd_ref[1], pb[...])
    own = (
        dot(fwd_ref[0, :, 0:256], db[0, 0:256, :])
        + dot(fwd_ref[1, :, 0:256], db[0, 0:256, :])
        + dot(fwd_ref[0, :, 0:256], db[1, 0:256, :])
    )
    held[...] = own
    ahead = dot(fwd_ref[0, :, 256:DEPTH], db[0, 256:DEPTH, :]) + dot(
        fwd_ref[1, :, 256:DEPTH], db[0, 256:DEPTH, :]
    )
    ahead = held[...] + ahead
    kr, ki = kernel[:HALF], kernel[HALF:]
    pr, pi = product[:HALF], product[HALF:]
    dr, di = ahead[:HALF], ahead[HALF:]
    zeros = jnp.zeros((DEPTH - POINTS, BLOCK), F32)
    mixed = jnp.concatenate([kr * pr - ki * pi, kr * pi + ki * pr, zeros], axis=0)
    mixed = wide_dot(inv_ref, slice(128, POINTS), whole, mixed)
    spread = jnp.concatenate([kr * dr + ki * di, kr * di - ki * dr, zeros], axis=0)
    spread = wide_dot(inv_ref, slice(0, end), whole, spread)
    for h in range(halves):
        z2[h] = mixed[:, lanes_of(h)]
        w2[h] = spread[:, lanes_of(h)]
    dr, di = held[:HALF, :], held[HALF:, :]
    lagged = jnp.concatenate([dr * pr + di * pi, dr * pi - di * pr, zeros], axis=0)
    lagged = wide_dot(lag_ref, whole, whole, lagged)
    medium_out[...] = (lagged * (damping * (2.0 / POINTS * norm_factor))).astype(BF16)

    for h in range(halves):
        lanes = lanes_of(h)
        sw = [[sw_ref[j, p, lanes][None, :] for j in range(3)] for p in range(3)]
        mw = [[mw_ref[j, p, lanes][None, :] for j in range(3)] for p in range(3)]
        sf = [sf_ref[j, lanes][None, :] for j in range(7)]
        for t, n in chunks(0, end):
            at = pl.ds(t, n)
            grad = w2[h, at, :]
            d[0, at, :] = gx[h, at, :] * z2[h, at, :]
            d[1, at, :] = grad * v2[h, at, :]
            d[2, at, :] = grad * k2[h, at, :]
        for t, n in chunks(0, end):
            at = pl.ds(t, n)
            if t < rows:
                mr_out[0, at, lanes] = weighted(d, (0,), t, n, mw[0], 1).astype(BF16)
                mr_out[1, at, lanes] = weighted(d, (1,), t, n, mw[1], 1).astype(BF16)
            grad = weighted(d, (2,), t, n, mw[2], 1)
            x[0, at, :] = grad * z1[h, at, :]
            x[3, at, :] = grad * q1[h, at, :]
        sums = [jnp.zeros((8, LANES), F32) for _ in range(7)]
        for t, n in chunks(0, end):
            at = pl.ds(t, n)
            grad = weighted(x, (3,), t, n, sf, 1)
            x[1, at, :] = grad * v1[h, at, :]
            x[2, at, :] = grad * k1[h, at, :]
            if t < rows:
                here = x[3, at, :]
                for j in range(7):
                    term = here * ps[h, pl.ds(PAD + t - j, n), :]
                    sums[j] = sums[j] + jnp.sum(term.reshape(n // 8, 8, LANES), axis=0)
        for j in range(7):
            tail[j : j + 1, :] = jnp.sum(sums[j], axis=0, keepdims=True)
        tail[7:8, :] = jnp.zeros((1, LANES), F32)
        short_out[:, lanes] = tail[0:8, :] * norm_factor
        for t, n in chunks(0, rows):
            for p in range(3):
                se_out[p, pl.ds(t, n), lanes] = weighted(x, (p,), t, n, sw[p], 1).astype(BF16)


def rows_of(*dims):
    return pl.BlockSpec(dims + (BLOCK,), lambda i: (0,) * len(dims) + (i,))


def fixed(array):
    return pl.BlockSpec(array.shape, lambda i: (0,) * array.ndim)


def f32_rows(*dims):
    return pltpu.VMEM(dims + (LANES,), F32)


def edges(se, mr, g, sw, mw, sf):
    rows, channels = g.shape
    return pl.pallas_call(
        edge_kernel,
        grid=(channels // BLOCK,),
        in_specs=[
            rows_of(3, rows),
            rows_of(2, rows),
            rows_of(rows),
            rows_of(3, 3),
            rows_of(3, 3),
            rows_of(7),
        ],
        out_specs=[rows_of(160), rows_of(176)],
        out_shape=[
            jax.ShapeDtypeStruct((160, channels), BF16),
            jax.ShapeDtypeStruct((176, channels), BF16),
        ],
        scratch_shapes=[
            f32_rows(5, 176),
            f32_rows(176),
            f32_rows(176),
            f32_rows(176),
            f32_rows(32),
        ],
        compiler_params=pltpu.CompilerParams(vmem_limit_bytes=32 * 2**20),
        cost_estimate=pl.CostEstimate(
            flops=60 * 144 * channels, bytes_accessed=7 * rows * channels, transcendentals=0
        ),
        name="edges",
    )(se, mr, g, sw, mw, sf)


def operators(norm_factor, se, mr, g, on, back, sw, mw, sf, mf, rate, tables):
    rows, channels = g.shape
    end = rows + REACH
    tables = [jnp.asarray(table) for table in tables]
    return pl.pallas_call(
        functools.partial(main_kernel, norm_factor),
        grid=(channels // BLOCK,),
        in_specs=[
            rows_of(3, rows),
            rows_of(2, rows),
            rows_of(rows),
            rows_of(160),
            rows_of(176),
            rows_of(3, 3),
            rows_of(3, 3),
            rows_of(7),
            rows_of(128),
            rows_of(1),
        ]
        + [fixed(table) for table in tables],
        out_specs=[rows_of(3, rows), rows_of(2, rows), rows_of(8), rows_of(128)],
        out_shape=[
            jax.ShapeDtypeStruct((3, rows, channels), BF16),
            jax.ShapeDtypeStruct((2, rows, channels), BF16),
            jax.ShapeDtypeStruct((8, channels), F32),
            jax.ShapeDtypeStruct((128, channels), BF16),
        ],
        scratch_shapes=[
            f32_rows(5, PAD + end),
            f32_rows(2, end),
            f32_rows(2, end),
            f32_rows(2, end),
            f32_rows(2, end),
            f32_rows(2, PAD + end),
            f32_rows(2, end),
            f32_rows(PAD + end),
            f32_rows(2, end),
            f32_rows(2, end),
            f32_rows(32),
            pltpu.VMEM((DEPTH, BLOCK), BF16),
            pltpu.VMEM((2, DEPTH, BLOCK), BF16),
            f32_rows(2, end),
            f32_rows(2, end),
            f32_rows(3, PAD + end),
            pltpu.VMEM((POINTS, BLOCK), F32),
        ],
        compiler_params=pltpu.CompilerParams(vmem_limit_bytes=48 * 2**20),
        cost_estimate=pl.CostEstimate(
            flops=4000 * rows * channels, bytes_accessed=20 * rows * channels, transcendentals=0
        ),
        name="operators",
    )(se, mr, g, on, back, sw, mw, sf, mf, rate, *tables)


def ctx_sums(short_rows, medium_part):
    count = lax.axis_size("ctx")
    channels = short_rows.shape[1]
    medium_length = medium_part.shape[0]
    depth = medium_length // count
    width = short_rows.size // (count * depth)
    terms = jnp.concatenate(
        [
            medium_part.reshape(count, depth, channels),
            short_rows.astype(BF16).reshape(count, depth, width),
        ],
        axis=2,
    )
    shares = lax.all_to_all(terms, "ctx", 0, 0, tiled=True)
    total = jnp.sum(shares.astype(F32), axis=0).astype(BF16)
    copies = jnp.broadcast_to(total[None], (count,) + total.shape)
    totals = lax.all_to_all(copies, "ctx", 0, 0, tiled=True).astype(F32)
    medium_total = totals[:, :, :channels].reshape(medium_length, channels)
    short_total = totals[:, :, channels:].reshape(short_rows.shape)[:7]
    return short_total, medium_total


def local(tables, se_input, mr_input, g, se_taps, mr_taps, sf, mf, decay_rate):
    rows, channels = g.shape
    count = lax.axis_size("ctx")
    norm_factor = 1.0 / math.sqrt(rows * count)
    se = jnp.transpose(se_input, (1, 0, 2))
    mr = jnp.transpose(mr_input, (1, 0, 2))
    on, back = edges(se, mr, g, se_taps, mr_taps, sf)
    on = lax.ppermute(on, "ctx", [(i, i + 1) for i in range(count - 1)])
    back = lax.ppermute(back, "ctx", [(i, i - 1) for i in range(1, count)])
    se_out, mr_out, short_rows, medium_part = operators(
        norm_factor, se, mr, g, on, back, se_taps, mr_taps, sf, mf, decay_rate[None, :], tables
    )
    short_total, medium_total = ctx_sums(short_rows, medium_part)
    return (
        jnp.transpose(se_out, (1, 0, 2)),
        jnp.transpose(mr_out, (1, 0, 2)),
        short_total,
        medium_total,
    )


def solution(mesh):
    tables = transform_tables()
    placed = (
        P("ctx", None, "ts"),
        P("ctx", None, "ts"),
        P("ctx", "ts"),
        P(None, None, "ts"),
        P(None, None, "ts"),
        P(None, "ts"),
        P(None, "ts"),
        P("ts"),
    )
    return jax.shard_map(
        functools.partial(local, tables),
        mesh=mesh,
        in_specs=placed,
        out_specs=(P("ctx", None, "ts"), P("ctx", None, "ts"), P(None, "ts"), P(None, "ts")),
        check_vma=False,
    )
```

```python
import functools
import math

import jax
import jax.numpy as jnp
import ml_dtypes
import numpy as np
from jax import lax
from jax.experimental import pallas as pl
from jax.experimental.pallas import tpu as pltpu
from jax.sharding import PartitionSpec as P

F32 = jnp.float32
BF16 = jnp.bfloat16
LANES = 128
BLOCK = 256
PAD = 16
REACH = 16
POINTS = 400
HALF = POINTS // 2
DEPTH = 512


def chunks(begin, end, step=32):
    return [(a, min(step, end - a)) for a in range(begin, end, step)]


def split(value):
    high = value.astype(BF16)
    return high, (value - high.astype(F32)).astype(BF16)


def transform_tables():
    frequency = (np.arange(HALF) + 0.5)[:, None]

    def table_at(places):
        angle = 2.0 * np.pi * frequency * places[None, :] / POINTS
        return np.concatenate([np.cos(angle), -np.sin(angle)], axis=0)

    forward = table_at(np.arange(POINTS))
    behind = table_at(np.concatenate([np.arange(-128, 0), np.arange(256, 256 + REACH)]))
    back = forward.T[: 256 + REACH]
    tables = []
    for table, depth in ((forward, DEPTH), (behind, 256), (back, DEPTH)):
        table = np.pad(table, ((0, 0), (0, depth - table.shape[1])))
        high = table.astype(ml_dtypes.bfloat16)
        low = (table - high.astype(np.float64)).astype(ml_dtypes.bfloat16)
        tables.append(np.stack([high, low]))
    return tables


def weighted(ref, lead, row, count, taps, step):
    total = ref[lead + (pl.ds(row, count), slice(None))] * taps[0]
    for j in range(1, len(taps)):
        total = total + ref[lead + (pl.ds(row + step * j, count), slice(None))] * taps[j]
    return total


def rounded(value):
    return value.astype(BF16).astype(F32)


def dot(a, b):
    return jnp.dot(a, b, preferred_element_type=F32)


def wide_dot(table, rows, columns, value):
    high, low = split(value)
    return (
        dot(table[0, rows, columns], high)
        + dot(table[1, rows, columns], high)
        + dot(table[0, rows, columns], low)
    )


def lanes_of(h):
    return slice(h * LANES, (h + 1) * LANES)


def feature_taps(ref, lanes):
    return [[ref[j, p, lanes][None, :] for j in range(3)] for p in range(3)]


def short_taps(ref, lanes):
    return [ref[j, lanes][None, :] for j in range(7)]


def product_of(first, second, conjugate):
    fr, fi = first[:HALF, :], first[HALF:, :]
    sr, si = second[:HALF, :], second[HALF:, :]
    zeros = jnp.zeros((DEPTH - POINTS, BLOCK), F32)
    if conjugate:
        return jnp.concatenate([fr * sr + fi * si, fr * si - fi * sr, zeros], axis=0)
    return jnp.concatenate([fr * sr - fi * si, fr * si + fi * sr, zeros], axis=0)


def edge_kernel(
    se_start, se_end, mr_start, mr_end, g_ref, sw_ref, mw_ref, sf_ref, last_ref, first_ref, x, q1, ps, y1, tail
):
    for h in range(g_ref.shape[1] // LANES):
        lanes = lanes_of(h)
        sw = feature_taps(sw_ref, lanes)
        mw = feature_taps(mw_ref, lanes)
        sf = short_taps(sf_ref, lanes)
        x[3, 0:PAD, :] = jnp.zeros((PAD, LANES), F32)
        for a, n in chunks(0, 144):
            x[3, pl.ds(PAD + a, n), :] = mr_start[0, pl.ds(a, n), lanes].astype(F32)
        for a, n in chunks(0, 144):
            q2 = weighted(x, (3,), PAD + a, n, mw[0], -1)
            first_ref[pl.ds(a, n), lanes] = (
                g_ref[pl.ds(a, n), lanes].astype(F32) * q2
            ).astype(BF16)
        for p in range(3):
            x[p, 0:16, :] = se_start[p, :, lanes].astype(F32)
        x[4, 0:16, :] = mr_start[1, 0:16, lanes].astype(F32)
        y1[0:16, :] = g_ref[0:16, lanes].astype(F32)
        tail[...] = jnp.zeros((32, LANES), F32)
        tail[0:2, :] = y1[0:2, :]
        tail[2:4, :] = x[3, PAD : PAD + 2, :]
        tail[4:14, :] = x[4, 0:10, :]
        tail[14:22, :] = x[0, 0:8, :]
        tail[22:24, :] = x[1, 0:2, :]
        tail[24:26, :] = x[2, 0:2, :]
        first_ref[144:176, lanes] = tail[...].astype(BF16)

        for p in range(3):
            x[p, 0:32, :] = se_end[p, :, lanes].astype(F32)
        for p in range(2):
            x[3 + p, 0:32, :] = mr_end[p, :, lanes].astype(F32)
        k1 = weighted(x, (1,), 8, 24, sw[1], -1)
        v1 = weighted(x, (2,), 8, 24, sw[2], -1)
        ps[8:32, :] = rounded(k1 * v1)
        q1[8:32, :] = weighted(x, (0,), 8, 24, sw[0], -1)
        y1[16:32, :] = rounded(q1[16:32, :] * weighted(ps, (), 16, 16, sf, -1))
        tail[...] = jnp.zeros((32, LANES), F32)
        tail[0:6, :] = ps[26:32, :]
        tail[6:8, :] = y1[30:32, :]
        for p in range(5):
            tail[8 + 2 * p : 10 + 2 * p, :] = x[p, 30:32, :]
        last_ref[:, lanes] = tail[...].astype(BF16)


def medium_spectrum(mf_ref, rate_ref, fwd_ref):
    lag = lax.broadcasted_iota(jnp.int32, (128, BLOCK), 0).astype(F32)
    damping = jnp.exp(-rate_ref[...] * lag) * (2.0 / POINTS)
    return damping, wide_dot(fwd_ref, slice(None), slice(0, 128), mf_ref[...] * damping)


def forward_kernel(
    se_ref,
    mr_ref,
    g_ref,
    before_ref,
    sw_ref,
    mw_ref,
    sf_ref,
    fwd_ref,
    feats,
    ps_ref,
    pb,
    own_d,
    x,
    ps,
    y1,
    tail,
    db,
):
    rows = se_ref.shape[1]
    for h in range(BLOCK // LANES):
        lanes = lanes_of(h)
        sw = feature_taps(sw_ref, lanes)
        mw = feature_taps(mw_ref, lanes)
        sf = short_taps(sf_ref, lanes)
        tail[...] = before_ref[:, lanes].astype(F32)
        ps[PAD - 6 : PAD, :] = tail[0:6, :]
        y1[PAD - 2 : PAD, :] = tail[6:8, :]
        for p in range(5):
            x[p, PAD - 2 : PAD, :] = tail[8 + 2 * p : 10 + 2 * p, :]
        for t, n in chunks(0, rows):
            for p in range(3):
                x[p, pl.ds(PAD + t, n), :] = se_ref[p, pl.ds(t, n), lanes].astype(F32)
            for p in range(2):
                x[3 + p, pl.ds(PAD + t, n), :] = mr_ref[p, pl.ds(t, n), lanes].astype(F32)
        for t, n in chunks(0, rows):
            r, at = PAD + t, pl.ds(t, n)
            key = weighted(x, (1,), r, n, sw[1], -1)
            value = weighted(x, (2,), r, n, sw[2], -1)
            product = (key * value).astype(BF16)
            ps_ref[at, lanes] = product
            ps[pl.ds(r, n), :] = product.astype(F32)
            query = weighted(x, (0,), r, n, sw[0], -1)
            feats[0, at, lanes] = query
            mixed = weighted(ps, (), r, n, sf, -1)
            feats[1, at, lanes] = mixed
            y1[pl.ds(r, n), :] = rounded(query * mixed)
            key = weighted(x, (4,), r, n, mw[1], -1)
            value = weighted(y1, (), r, n, mw[2], -1)
            feats[2, at, lanes] = key
            feats[3, at, lanes] = value
            pb[at, lanes] = (key * value).astype(BF16)
            query = weighted(x, (3,), r, n, mw[0], -1)
            high, low = split(g_ref[at, lanes].astype(F32) * query)
            db[0, at, lanes] = high
            db[1, at, lanes] = low
    own = slice(0, 256)
    own_d[...] = (
        dot(fwd_ref[0, :, own], db[0])
        + dot(fwd_ref[1, :, own], db[0])
        + dot(fwd_ref[0, :, own], db[1])
    )


def middle_kernel(
    norm_factor,
    feats,
    ps_ref,
    pb,
    own_d,
    mf_ref,
    rate_ref,
    before_ref,
    last_ref,
    ahead_ref,
    sw_ref,
    mw_ref,
    sf_ref,
    fwd_ref,
    inv_ref,
    medium_out,
    short_out,
    w2_out,
    dy1_out,
    feats_out,
    product_out,
    x,
    ps,
    y1,
    tail,
    db,
    d,
    dz,
):
    rows = feats.shape[1]
    top = lax.broadcasted_iota(jnp.int32, (REACH, LANES), 0) < 2
    here = pl.ds(PAD, REACH)
    for h in range(BLOCK // LANES):
        lanes = lanes_of(h)
        sw = feature_taps(sw_ref, lanes)
        mw = feature_taps(mw_ref, lanes)
        sf = short_taps(sf_ref, lanes)
        tail[...] = last_ref[:, lanes].astype(F32)
        ps[PAD - 6 : PAD, :] = tail[0:6, :]
        y1[PAD - 2 : PAD, :] = tail[6:8, :]
        for p in range(5):
            x[p, PAD - 2 : PAD, :] = tail[8 + 2 * p : 10 + 2 * p, :]
            x[p, here, :] = jnp.zeros((REACH, LANES), F32)
        tail[...] = ahead_ref[144:176, lanes].astype(F32)
        x[3, PAD : PAD + 2, :] = tail[2:4, :]
        x[4, PAD : PAD + 10, :] = tail[4:14, :]
        x[0, PAD : PAD + 8, :] = tail[14:22, :]
        x[1, PAD : PAD + 2, :] = tail[22:24, :]
        x[2, PAD : PAD + 2, :] = tail[24:26, :]
        query = weighted(x, (0,), PAD, REACH, sw[0], -1)
        key = weighted(x, (1,), PAD, REACH, sw[1], -1)
        value = weighted(x, (2,), PAD, REACH, sw[2], -1)
        feats_out[0, :, lanes] = query
        feats_out[4, :, lanes] = key
        feats_out[5, :, lanes] = value
        ps[here, :] = rounded(key * value)
        mixed = weighted(ps, (), PAD, REACH, sf, -1)
        feats_out[1, :, lanes] = mixed
        y1[here, :] = rounded(query * mixed)
        key = weighted(x, (4,), PAD, REACH, mw[1], -1)
        value = weighted(y1, (), PAD, REACH, mw[2], -1)
        feats_out[2, :, lanes] = key
        feats_out[3, :, lanes] = value
        product_out[:, lanes] = jnp.where(top, key * value, 0.0).astype(BF16)
        upstream = tail[0:REACH, :] * weighted(x, (3,), PAD, REACH, mw[0], -1)
        upstream = jnp.where(top, upstream, ahead_ref[0:REACH, lanes].astype(F32))
        db[0:REACH, lanes] = upstream.astype(BF16)
        db[REACH : POINTS - 256, lanes] = ahead_ref[REACH : POINTS - 256, lanes]
        db[POINTS - 256 : 256, lanes] = jnp.zeros((DEPTH - POINTS, LANES), BF16)

    beyond = slice(256, DEPTH)
    damping, kernel = medium_spectrum(mf_ref, rate_ref, fwd_ref)
    own = slice(0, 256)
    pp = dot(fwd_ref[0, :, own], pb[...]) + dot(fwd_ref[1, :, own], pb[...])
    dd = own_d[...] + (dot(fwd_ref[0, :, beyond], db[...]) + dot(fwd_ref[1, :, beyond], db[...]))
    spread = wide_dot(inv_ref, slice(None), slice(None), product_of(kernel, dd, True))
    w2_out[...] = spread
    lagged = wide_dot(inv_ref, slice(0, 128), slice(None), product_of(pp, dd, True))
    medium_out[...] = (lagged * (damping * norm_factor)).astype(BF16)

    for h in range(BLOCK // LANES):
        lanes = lanes_of(h)
        mw = feature_taps(mw_ref, lanes)
        tail[...] = before_ref[:, lanes].astype(F32)
        ps[PAD - 6 : PAD, :] = tail[0:6, :]
        for t, n in chunks(0, rows):
            at = pl.ds(t, n)
            ps[pl.ds(PAD + t, n), :] = ps_ref[at, lanes].astype(F32)
            d[at, :] = w2_out[at, lanes] * feats[2, at, lanes]
        last = pl.ds(rows, REACH)
        d[last, :] = w2_out[last, lanes] * feats_out[2, :, lanes]
        d[rows + REACH : rows + REACH + 8, :] = jnp.zeros((8, LANES), F32)
        dy1_out[last, lanes] = weighted(d, (), rows, REACH, mw[2], 1)
        sums = [jnp.zeros((8, LANES), F32) for _ in range(7)]
        for t, n in chunks(0, rows):
            at = pl.ds(t, n)
            grad = weighted(d, (), t, n, mw[2], 1)
            dy1_out[at, lanes] = grad
            grad = grad * feats[0, at, lanes]
            for j in range(7):
                term = grad * ps[pl.ds(PAD + t - j, n), :]
                sums[j] = sums[j] + jnp.sum(term.reshape(n // 8, 8, LANES), axis=0)
        for j in range(7):
            tail[j : j + 1, :] = jnp.sum(sums[j], axis=0, keepdims=True)
        tail[7:8, :] = jnp.zeros((1, LANES), F32)
        short_out[:, lanes] = tail[0:8, :] * norm_factor


def backward_kernel(
    feats,
    feats_ahead,
    w2,
    dy1,
    own_ref,
    mf_ref,
    rate_ref,
    behind_ref,
    product_ref,
    se_ref,
    before_ref,
    g_ref,
    ahead_ref,
    sw_ref,
    mw_ref,
    sf_ref,
    fwd_ref,
    rim_ref,
    inv_ref,
    se_out,
    mr_out,
    x,
    pb,
    z2,
    tail,
    d,
    e,
    dz,
):
    rows = feats.shape[1]
    pb[0:128, :] = behind_ref[...]
    pb[128 : 128 + REACH, :] = product_ref[...]
    pb[128 + REACH : 256, :] = jnp.zeros((128 - REACH, BLOCK), BF16)
    _, kernel = medium_spectrum(mf_ref, rate_ref, fwd_ref)
    own = slice(0, 256)
    pp = (
        dot(fwd_ref[0, :, own], own_ref[...])
        + dot(fwd_ref[1, :, own], own_ref[...])
        + dot(rim_ref[0], pb[...])
        + dot(rim_ref[1], pb[...])
    )
    z2[...] = wide_dot(inv_ref, slice(None), slice(None), product_of(kernel, pp, False))
    spans = [(feats, 0, t, n) for t, n in chunks(0, rows)] + [(feats_ahead, rows, rows, REACH)]
    for h in range(BLOCK // LANES):
        lanes = lanes_of(h)
        sw = feature_taps(sw_ref, lanes)
        mw = feature_taps(mw_ref, lanes)
        sf = short_taps(sf_ref, lanes)
        tail[...] = before_ref[:, lanes].astype(F32)
        for p in range(2):
            x[p, PAD - 2 : PAD, :] = tail[10 + 2 * p : 12 + 2 * p, :]
            for t, n in chunks(0, rows):
                x[p, pl.ds(PAD + t, n), :] = se_ref[1 + p, pl.ds(t, n), lanes].astype(F32)
        tail[...] = ahead_ref[144:176, lanes].astype(F32)
        tail[2:16, :] = jnp.zeros((14, LANES), F32)
        for source, base, t, n in spans:
            at, own = pl.ds(t, n), pl.ds(t - base, n)
            grad = w2[at, lanes]
            d[1, at, :] = grad * source[3, own, lanes]
            upstream = tail[0:REACH, :] if base else g_ref[at, lanes].astype(F32)
            d[0, at, :] = upstream * z2[at, lanes]
            grad = dy1[at, lanes]
            e[0, at, :] = grad * source[1, own, lanes]
            dz[at, :] = grad * source[0, own, lanes]
        for source, base, t, n in spans:
            at, own = pl.ds(t, n), pl.ds(t - base, n)
            grad = weighted(dz, (), t, n, sf, 1)
            if base:
                key, value = source[4, own, lanes], source[5, own, lanes]
            else:
                key = weighted(x, (0,), PAD + t, n, sw[1], -1)
                value = weighted(x, (1,), PAD + t, n, sw[2], -1)
            e[1, at, :] = grad * value
            e[2, at, :] = grad * key
        for t, n in chunks(0, rows):
            at = pl.ds(t, n)
            for p in range(2):
                mr_out[p, at, lanes] = weighted(d, (p,), t, n, mw[p], 1).astype(BF16)
            for p in range(3):
                se_out[p, at, lanes] = weighted(e, (p,), t, n, sw[p], 1).astype(BF16)


def rows_of(*dims):
    return pl.BlockSpec(dims + (BLOCK,), lambda i: (0,) * len(dims) + (i,))


def fixed(array):
    return pl.BlockSpec(array.shape, lambda i: (0,) * array.ndim)


def f32_rows(*dims):
    return pltpu.VMEM(dims + (LANES,), F32)


def bf16_rows(*dims):
    return pltpu.VMEM(dims + (BLOCK,), BF16)


def blocks_call(name, body, arrays, tables, outs, scratch, flops):
    channels = arrays[0].shape[-1]
    return pl.pallas_call(
        body,
        grid=(channels // BLOCK,),
        in_specs=[rows_of(*a.shape[:-1]) for a in arrays] + [fixed(t) for t in tables],
        out_specs=[rows_of(*dims) for dims, _ in outs],
        out_shape=[jax.ShapeDtypeStruct(dims + (channels,), kind) for dims, kind in outs],
        scratch_shapes=scratch,
        compiler_params=pltpu.CompilerParams(vmem_limit_bytes=56 * 2**20),
        cost_estimate=pl.CostEstimate(
            flops=flops * 256 * channels, bytes_accessed=16 * 256 * channels, transcendentals=0
        ),
        name=name,
    )(*arrays, *tables)


def edges(se, mr, g, sw, mw, sf):
    rows, channels = g.shape
    wide = min(channels, 512)

    def part(lead, count, at):
        zeros = (0,) * len(lead)
        return pl.BlockSpec(lead + (count, wide), lambda i: zeros + (at, i))

    return pl.pallas_call(
        edge_kernel,
        grid=(channels // wide,),
        in_specs=[
            part((3,), 16, 0),
            part((3,), 32, rows // 32 - 1),
            part((2,), 144, 0),
            part((2,), 32, rows // 32 - 1),
            part((), 144, 0),
            part((3,), 3, 0),
            part((3,), 3, 0),
            part((), 7, 0),
        ],
        out_specs=[part((), 32, 0), part((), 176, 0)],
        out_shape=[
            jax.ShapeDtypeStruct((32, channels), BF16),
            jax.ShapeDtypeStruct((176, channels), BF16),
        ],
        scratch_shapes=[
            f32_rows(5, 160),
            f32_rows(32),
            f32_rows(32),
            f32_rows(32),
            f32_rows(32),
        ],
        compiler_params=pltpu.CompilerParams(vmem_limit_bytes=56 * 2**20),
        name="edges",
    )(se, se, mr, mr, g, sw, mw, sf)


def ctx_sums(short_rows, medium_part):
    count = lax.axis_size("ctx")
    channels = short_rows.shape[1]
    medium_length = medium_part.shape[0]
    depth = medium_length // count
    width = short_rows.size // (count * depth)
    terms = jnp.concatenate(
        [
            medium_part.reshape(count, depth, channels),
            short_rows.astype(BF16).reshape(count, depth, width),
        ],
        axis=2,
    )
    shares = lax.all_to_all(terms, "ctx", 0, 0, tiled=True)
    total = jnp.sum(shares.astype(F32), axis=0).astype(BF16)
    copies = jnp.broadcast_to(total[None], (count,) + total.shape)
    totals = lax.all_to_all(copies, "ctx", 0, 0, tiled=True).astype(F32)
    medium_total = totals[:, :, :channels].reshape(medium_length, channels)
    short_total = totals[:, :, channels:].reshape(short_rows.shape)[:7]
    return short_total, medium_total


def local(tables, se_input, mr_input, g, sw, mw, sf, mf, decay_rate):
    rows, channels = g.shape
    end = rows + REACH
    count = lax.axis_size("ctx")
    norm_factor = 1.0 / math.sqrt(rows * count)
    fwd, rim, inv = (jnp.asarray(table) for table in tables)
    se = jnp.transpose(se_input, (1, 0, 2))
    mr = jnp.transpose(mr_input, (1, 0, 2))
    onward = [(i, i + 1) for i in range(count - 1)]
    backward = [(i, i - 1) for i in range(1, count)]
    rate = decay_rate[None, :]

    last, first = edges(se, mr, g, sw, mw, sf)
    before = lax.ppermute(last, "ctx", onward)
    ahead = lax.ppermute(first, "ctx", backward)
    feats, ps, product, own_d = blocks_call(
        "forward",
        forward_kernel,
        [se, mr, g, before, sw, mw, sf],
        [fwd],
        [
            ((4, rows), F32),
            ((rows,), BF16),
            ((rows,), BF16),
            ((POINTS,), F32),
        ],
        [
            f32_rows(5, PAD + rows),
            f32_rows(PAD + rows),
            f32_rows(PAD + rows),
            f32_rows(32),
            bf16_rows(2, rows),
        ],
        4000,
    )
    behind = lax.ppermute(product[rows - 128 :], "ctx", onward)
    medium_part, short_rows, w2, dy1, feats_ahead, product_ahead = blocks_call(
        "middle",
        functools.partial(middle_kernel, norm_factor),
        [feats, ps, product, own_d, mf, rate, before, last, ahead, sw, mw, sf],
        [fwd, inv],
        [
            ((128,), BF16),
            ((8,), F32),
            ((end,), F32),
            ((end,), F32),
            ((6, REACH), F32),
            ((REACH,), BF16),
        ],
        [
            f32_rows(5, 32),
            f32_rows(PAD + rows),
            f32_rows(32),
            f32_rows(32),
            bf16_rows(256),
            f32_rows(end + 16),
            f32_rows(end + 16),
        ],
        4000,
    )
    medium_part, behind = lax.optimization_barrier((medium_part, behind))
    se_out, mr_out = blocks_call(
        "backward",
        backward_kernel,
        [
            feats,
            feats_ahead,
            w2,
            dy1,
            product,
            mf,
            rate,
            behind,
            product_ahead,
            se,
            before,
            g,
            ahead,
            sw,
            mw,
            sf,
        ],
        [fwd, rim, inv],
        [((3, rows), BF16), ((2, rows), BF16)],
        [
            f32_rows(2, PAD + rows),
            bf16_rows(256),
            pltpu.VMEM((end, BLOCK), F32),
            f32_rows(32),
            f32_rows(2, end + 16),
            f32_rows(3, end + 16),
            f32_rows(end + 16),
        ],
        4000,
    )
    short_total, medium_total = ctx_sums(short_rows, medium_part)
    return (
        jnp.transpose(se_out, (1, 0, 2)),
        jnp.transpose(mr_out, (1, 0, 2)),
        short_total,
        medium_total,
    )


def solution(mesh):
    tables = transform_tables()
    placed = (
        P("ctx", None, "ts"),
        P("ctx", None, "ts"),
        P("ctx", "ts"),
        P(None, None, "ts"),
        P(None, None, "ts"),
        P(None, "ts"),
        P(None, "ts"),
        P("ts"),
    )
    return jax.shard_map(
        functools.partial(local, tables),
        mesh=mesh,
        in_specs=placed,
        out_specs=(P("ctx", None, "ts"), P("ctx", None, "ts"), P(None, "ts"), P(None, "ts")),
        check_vma=False,
    )
```

```python
import functools
import math

import jax
import jax.numpy as jnp
import ml_dtypes
import numpy as np
from jax import lax
from jax.experimental import pallas as pl
from jax.experimental.pallas import tpu as pltpu
from jax.sharding import PartitionSpec as P

F32 = jnp.float32
BF16 = jnp.bfloat16
LANES = 128
BLOCK = 256
PAD = 16
REACH = 16
POINTS = 400
HALF = POINTS // 2
DEPTH = 512


def chunks(begin, end, step=32):
    return [(a, min(step, end - a)) for a in range(begin, end, step)]


def split(value):
    high = value.astype(BF16)
    return high, (value - high.astype(F32)).astype(BF16)


def transform_tables():
    frequency = (np.arange(HALF) + 0.5)[:, None]

    def table_at(places):
        angle = 2.0 * np.pi * frequency * places[None, :] / POINTS
        return np.concatenate([np.cos(angle), -np.sin(angle)], axis=0)

    forward = table_at(np.arange(POINTS))
    behind = table_at(np.concatenate([np.arange(-128, 0), np.arange(256, 256 + REACH)]))
    back = forward.T[: 256 + REACH]
    tables = []
    for table, depth in ((forward, DEPTH), (behind, 256), (back, DEPTH)):
        table = np.pad(table, ((0, 0), (0, depth - table.shape[1])))
        high = table.astype(ml_dtypes.bfloat16)
        low = (table - high.astype(np.float64)).astype(ml_dtypes.bfloat16)
        tables.append(np.stack([high, low]))
    return tables


def weighted(ref, lead, row, count, taps, step):
    total = ref[lead + (pl.ds(row, count), slice(None))] * taps[0]
    for j in range(1, len(taps)):
        total = total + ref[lead + (pl.ds(row + step * j, count), slice(None))] * taps[j]
    return total


def rounded(value):
    return value.astype(BF16).astype(F32)


def dot(a, b):
    return jnp.dot(a, b, preferred_element_type=F32)


def wide_dot(table, rows, columns, value):
    high, low = split(value)
    return (
        dot(table[0, rows, columns], high)
        + dot(table[1, rows, columns], high)
        + dot(table[0, rows, columns], low)
    )


def lanes_of(h):
    return slice(h * LANES, (h + 1) * LANES)


def feature_taps(ref, lanes):
    return [[ref[j, p, lanes][None, :] for j in range(3)] for p in range(3)]


def short_taps(ref, lanes):
    return [ref[j, lanes][None, :] for j in range(7)]


def product_of(first, second, conjugate):
    fr, fi = first[:HALF, :], first[HALF:, :]
    sr, si = second[:HALF, :], second[HALF:, :]
    zeros = jnp.zeros((DEPTH - POINTS, BLOCK), F32)
    if conjugate:
        return jnp.concatenate([fr * sr + fi * si, fr * si - fi * sr, zeros], axis=0)
    return jnp.concatenate([fr * sr - fi * si, fr * si + fi * sr, zeros], axis=0)


def edge_kernel(
    se_start, se_end, mr_start, mr_end, g_ref, sw_ref, mw_ref, sf_ref, last_ref, first_ref, x, q1, ps, y1, tail
):
    for h in range(g_ref.shape[1] // LANES):
        lanes = lanes_of(h)
        sw = feature_taps(sw_ref, lanes)
        mw = feature_taps(mw_ref, lanes)
        sf = short_taps(sf_ref, lanes)
        x[3, 0:PAD, :] = jnp.zeros((PAD, LANES), F32)
        for a, n in chunks(0, 144):
            x[3, pl.ds(PAD + a, n), :] = mr_start[0, pl.ds(a, n), lanes].astype(F32)
        for a, n in chunks(0, 144):
            q2 = weighted(x, (3,), PAD + a, n, mw[0], -1)
            first_ref[pl.ds(a, n), lanes] = (
                g_ref[pl.ds(a, n), lanes].astype(F32) * q2
            ).astype(BF16)
        for p in range(3):
            x[p, 0:16, :] = se_start[p, :, lanes].astype(F32)
        x[4, 0:16, :] = mr_start[1, 0:16, lanes].astype(F32)
        y1[0:16, :] = g_ref[0:16, lanes].astype(F32)
        tail[...] = jnp.zeros((32, LANES), F32)
        tail[0:2, :] = y1[0:2, :]
        tail[2:4, :] = x[3, PAD : PAD + 2, :]
        tail[4:14, :] = x[4, 0:10, :]
        tail[14:22, :] = x[0, 0:8, :]
        tail[22:24, :] = x[1, 0:2, :]
        tail[24:26, :] = x[2, 0:2, :]
        first_ref[144:176, lanes] = tail[...].astype(BF16)

        for p in range(3):
            x[p, 0:32, :] = se_end[p, :, lanes].astype(F32)
        for p in range(2):
            x[3 + p, 0:32, :] = mr_end[p, :, lanes].astype(F32)
        k1 = weighted(x, (1,), 8, 24, sw[1], -1)
        v1 = weighted(x, (2,), 8, 24, sw[2], -1)
        ps[8:32, :] = rounded(k1 * v1)
        q1[8:32, :] = weighted(x, (0,), 8, 24, sw[0], -1)
        y1[16:32, :] = rounded(q1[16:32, :] * weighted(ps, (), 16, 16, sf, -1))
        tail[...] = jnp.zeros((32, LANES), F32)
        tail[0:6, :] = ps[26:32, :]
        tail[6:8, :] = y1[30:32, :]
        for p in range(5):
            tail[8 + 2 * p : 10 + 2 * p, :] = x[p, 30:32, :]
        last_ref[:, lanes] = tail[...].astype(BF16)


def medium_spectrum(mf_ref, rate_ref, fwd_ref):
    lag = lax.broadcasted_iota(jnp.int32, (128, BLOCK), 0).astype(F32)
    damping = jnp.exp(-rate_ref[...] * lag) * (2.0 / POINTS)
    return damping, wide_dot(fwd_ref, slice(None), slice(0, 128), mf_ref[...] * damping)


def forward_kernel(
    se_ref,
    mr_ref,
    g_ref,
    before_ref,
    sw_ref,
    mw_ref,
    sf_ref,
    fwd_ref,
    q1_ref,
    z1_ref,
    k2_ref,
    v2_ref,
    ps_ref,
    pb,
    own_d,
    x,
    ps,
    y1,
    tail,
    db,
):
    rows = se_ref.shape[1]
    for h in range(BLOCK // LANES):
        lanes = lanes_of(h)
        sw = feature_taps(sw_ref, lanes)
        mw = feature_taps(mw_ref, lanes)
        sf = short_taps(sf_ref, lanes)
        tail[...] = before_ref[:, lanes].astype(F32)
        ps[PAD - 6 : PAD, :] = tail[0:6, :]
        y1[PAD - 2 : PAD, :] = tail[6:8, :]
        for p in range(5):
            x[p, PAD - 2 : PAD, :] = tail[8 + 2 * p : 10 + 2 * p, :]
        for t, n in chunks(0, rows):
            for p in range(3):
                x[p, pl.ds(PAD + t, n), :] = se_ref[p, pl.ds(t, n), lanes].astype(F32)
            for p in range(2):
                x[3 + p, pl.ds(PAD + t, n), :] = mr_ref[p, pl.ds(t, n), lanes].astype(F32)
        for t, n in chunks(0, rows):
            r, at = PAD + t, pl.ds(t, n)
            key = weighted(x, (1,), r, n, sw[1], -1)
            value = weighted(x, (2,), r, n, sw[2], -1)
            product = (key * value).astype(BF16)
            ps_ref[at, lanes] = product
            ps[pl.ds(r, n), :] = product.astype(F32)
            query = weighted(x, (0,), r, n, sw[0], -1)
            q1_ref[at, lanes] = query
            mixed = weighted(ps, (), r, n, sf, -1)
            z1_ref[at, lanes] = mixed
            y1[pl.ds(r, n), :] = rounded(query * mixed)
            key = weighted(x, (4,), r, n, mw[1], -1)
            value = weighted(y1, (), r, n, mw[2], -1)
            k2_ref[at, lanes] = key
            v2_ref[at, lanes] = value
            pb[at, lanes] = (key * value).astype(BF16)
            query = weighted(x, (3,), r, n, mw[0], -1)
            high, low = split(g_ref[at, lanes].astype(F32) * query)
            db[0, at, lanes] = high
            db[1, at, lanes] = low
    own = slice(0, 256)
    own_d[...] = (
        dot(fwd_ref[0, :, own], db[0])
        + dot(fwd_ref[1, :, own], db[0])
        + dot(fwd_ref[0, :, own], db[1])
    )


def middle_kernel(
    norm_factor,
    q1_ref,
    k2_ref,
    ps_ref,
    pb,
    own_d,
    mf_ref,
    rate_ref,
    before_ref,
    last_ref,
    ahead_ref,
    sw_ref,
    mw_ref,
    sf_ref,
    fwd_ref,
    inv_ref,
    medium_out,
    short_out,
    w2_out,
    dy1_out,
    feats_out,
    v2_out,
    product_out,
    x,
    ps,
    y1,
    tail,
    db,
    d,
    dz,
):
    rows = q1_ref.shape[0]
    top = lax.broadcasted_iota(jnp.int32, (REACH, LANES), 0) < 2
    here = pl.ds(PAD, REACH)
    for h in range(BLOCK // LANES):
        lanes = lanes_of(h)
        sw = feature_taps(sw_ref, lanes)
        mw = feature_taps(mw_ref, lanes)
        sf = short_taps(sf_ref, lanes)
        tail[...] = last_ref[:, lanes].astype(F32)
        ps[PAD - 6 : PAD, :] = tail[0:6, :]
        y1[PAD - 2 : PAD, :] = tail[6:8, :]
        for p in range(5):
            x[p, PAD - 2 : PAD, :] = tail[8 + 2 * p : 10 + 2 * p, :]
            x[p, here, :] = jnp.zeros((REACH, LANES), F32)
        tail[...] = ahead_ref[144:176, lanes].astype(F32)
        x[3, PAD : PAD + 2, :] = tail[2:4, :]
        x[4, PAD : PAD + 10, :] = tail[4:14, :]
        x[0, PAD : PAD + 8, :] = tail[14:22, :]
        x[1, PAD : PAD + 2, :] = tail[22:24, :]
        x[2, PAD : PAD + 2, :] = tail[24:26, :]
        query = weighted(x, (0,), PAD, REACH, sw[0], -1)
        key = weighted(x, (1,), PAD, REACH, sw[1], -1)
        value = weighted(x, (2,), PAD, REACH, sw[2], -1)
        feats_out[0, :, lanes] = query
        feats_out[3, :, lanes] = key
        feats_out[4, :, lanes] = value
        ps[here, :] = rounded(key * value)
        mixed = weighted(ps, (), PAD, REACH, sf, -1)
        feats_out[1, :, lanes] = mixed
        y1[here, :] = rounded(query * mixed)
        key = weighted(x, (4,), PAD, REACH, mw[1], -1)
        value = weighted(y1, (), PAD, REACH, mw[2], -1)
        feats_out[2, :, lanes] = key
        v2_out[:, lanes] = value
        product_out[:, lanes] = jnp.where(top, key * value, 0.0).astype(BF16)
        upstream = tail[0:REACH, :] * weighted(x, (3,), PAD, REACH, mw[0], -1)
        upstream = jnp.where(top, upstream, ahead_ref[0:REACH, lanes].astype(F32))
        db[0:REACH, lanes] = upstream.astype(BF16)
        db[REACH : POINTS - 256, lanes] = ahead_ref[REACH : POINTS - 256, lanes]
        db[POINTS - 256 : 256, lanes] = jnp.zeros((DEPTH - POINTS, LANES), BF16)

    beyond = slice(256, DEPTH)
    damping, kernel = medium_spectrum(mf_ref, rate_ref, fwd_ref)
    own = slice(0, 256)
    pp = dot(fwd_ref[0, :, own], pb[...]) + dot(fwd_ref[1, :, own], pb[...])
    dd = own_d[...] + (dot(fwd_ref[0, :, beyond], db[...]) + dot(fwd_ref[1, :, beyond], db[...]))
    spread = wide_dot(inv_ref, slice(None), slice(None), product_of(kernel, dd, True))
    w2_out[...] = spread
    lagged = wide_dot(inv_ref, slice(0, 128), slice(None), product_of(pp, dd, True))
    medium_out[...] = (lagged * (damping * norm_factor)).astype(BF16)

    for h in range(BLOCK // LANES):
        lanes = lanes_of(h)
        mw = feature_taps(mw_ref, lanes)
        tail[...] = before_ref[:, lanes].astype(F32)
        ps[PAD - 6 : PAD, :] = tail[0:6, :]
        for t, n in chunks(0, rows):
            at = pl.ds(t, n)
            ps[pl.ds(PAD + t, n), :] = ps_ref[at, lanes].astype(F32)
            d[at, :] = w2_out[at, lanes] * k2_ref[at, lanes]
        last = pl.ds(rows, REACH)
        d[last, :] = w2_out[last, lanes] * feats_out[2, :, lanes]
        d[rows + REACH : rows + REACH + 8, :] = jnp.zeros((8, LANES), F32)
        dy1_out[last, lanes] = weighted(d, (), rows, REACH, mw[2], 1)
        sums = [jnp.zeros((8, LANES), F32) for _ in range(7)]
        for t, n in chunks(0, rows):
            at = pl.ds(t, n)
            grad = weighted(d, (), t, n, mw[2], 1)
            dy1_out[at, lanes] = grad
            grad = grad * q1_ref[at, lanes]
            for j in range(7):
                term = grad * ps[pl.ds(PAD + t - j, n), :]
                sums[j] = sums[j] + jnp.sum(term.reshape(n // 8, 8, LANES), axis=0)
        for j in range(7):
            tail[j : j + 1, :] = jnp.sum(sums[j], axis=0, keepdims=True)
        tail[7:8, :] = jnp.zeros((1, LANES), F32)
        short_out[:, lanes] = (tail[0:16, :] * norm_factor).astype(BF16)[0:8]


def spans(rows):
    return [(0, t, n) for t, n in chunks(0, rows)] + [(rows, rows, REACH)]


def se_backward_kernel(
    q1_ref, z1_ref, feats_ahead, dy1, se_ref, before_ref, sw_ref, sf_ref, se_out, x, tail, e, dz
):
    rows = q1_ref.shape[0]
    for h in range(BLOCK // LANES):
        lanes = lanes_of(h)
        sw = feature_taps(sw_ref, lanes)
        sf = short_taps(sf_ref, lanes)
        tail[...] = before_ref[:, lanes].astype(F32)
        for p in range(2):
            x[p, PAD - 2 : PAD, :] = tail[10 + 2 * p : 12 + 2 * p, :]
            for t, n in chunks(0, rows):
                x[p, pl.ds(PAD + t, n), :] = se_ref[1 + p, pl.ds(t, n), lanes].astype(F32)
        for base, t, n in spans(rows):
            at, own = pl.ds(t, n), pl.ds(t - base, n)
            grad = dy1[at, lanes]
            query = feats_ahead[0, own, lanes] if base else q1_ref[own, lanes]
            mixed = feats_ahead[1, own, lanes] if base else z1_ref[own, lanes]
            e[0, at, :] = grad * mixed
            dz[at, :] = grad * query
        for base, t, n in spans(rows):
            at, own = pl.ds(t, n), pl.ds(t - base, n)
            grad = weighted(dz, (), t, n, sf, 1)
            if base:
                key, value = feats_ahead[3, own, lanes], feats_ahead[4, own, lanes]
            else:
                key = weighted(x, (0,), PAD + t, n, sw[1], -1)
                value = weighted(x, (1,), PAD + t, n, sw[2], -1)
            e[1, at, :] = grad * value
            e[2, at, :] = grad * key
        for t, n in chunks(0, rows):
            at = pl.ds(t, n)
            for p in range(3):
                se_out[p, at, lanes] = weighted(e, (p,), t, n, sw[p], 1).astype(BF16)


def mr_backward_kernel(
    v2,
    v2_ahead,
    w2,
    own_ref,
    mf_ref,
    rate_ref,
    behind_ref,
    product_ref,
    g_ref,
    ahead_ref,
    mw_ref,
    fwd_ref,
    rim_ref,
    inv_ref,
    mr_out,
    pb,
    z2,
    tail,
    d,
):
    rows = v2.shape[0]
    pb[0:128, :] = behind_ref[...]
    pb[128 : 128 + REACH, :] = product_ref[...]
    pb[128 + REACH : 256, :] = jnp.zeros((128 - REACH, BLOCK), BF16)
    _, kernel = medium_spectrum(mf_ref, rate_ref, fwd_ref)
    own = slice(0, 256)
    pp = (
        dot(fwd_ref[0, :, own], own_ref[...])
        + dot(fwd_ref[1, :, own], own_ref[...])
        + dot(rim_ref[0], pb[...])
        + dot(rim_ref[1], pb[...])
    )
    z2[...] = wide_dot(inv_ref, slice(None), slice(None), product_of(kernel, pp, False))
    for h in range(BLOCK // LANES):
        lanes = lanes_of(h)
        mw = feature_taps(mw_ref, lanes)
        tail[...] = ahead_ref[144:176, lanes].astype(F32)
        tail[2:16, :] = jnp.zeros((14, LANES), F32)
        for base, t, n in spans(rows):
            at, own = pl.ds(t, n), pl.ds(t - base, n)
            value = v2_ahead[own, lanes] if base else v2[own, lanes]
            d[1, at, :] = w2[at, lanes] * value
            upstream = tail[0:REACH, :] if base else g_ref[at, lanes].astype(F32)
            d[0, at, :] = upstream * z2[at, lanes]
        for t, n in chunks(0, rows):
            for p in range(2):
                mr_out[p, pl.ds(t, n), lanes] = weighted(d, (p,), t, n, mw[p], 1).astype(BF16)


def rows_of(*dims):
    return pl.BlockSpec(dims + (BLOCK,), lambda i: (0,) * len(dims) + (i,))


def fixed(array):
    return pl.BlockSpec(array.shape, lambda i: (0,) * array.ndim)


def f32_rows(*dims):
    return pltpu.VMEM(dims + (LANES,), F32)


def bf16_rows(*dims):
    return pltpu.VMEM(dims + (BLOCK,), BF16)


def blocks_call(name, body, arrays, tables, outs, scratch, flops):
    channels = arrays[0].shape[-1]
    return pl.pallas_call(
        body,
        grid=(channels // BLOCK,),
        in_specs=[rows_of(*a.shape[:-1]) for a in arrays] + [fixed(t) for t in tables],
        out_specs=[rows_of(*dims) for dims, _ in outs],
        out_shape=[jax.ShapeDtypeStruct(dims + (channels,), kind) for dims, kind in outs],
        scratch_shapes=scratch,
        compiler_params=pltpu.CompilerParams(vmem_limit_bytes=56 * 2**20),
        cost_estimate=pl.CostEstimate(
            flops=flops * 256 * channels, bytes_accessed=16 * 256 * channels, transcendentals=0
        ),
        name=name,
    )(*arrays, *tables)


def edges(se, mr, g, sw, mw, sf):
    rows, channels = g.shape
    wide = min(channels, 512)

    def part(lead, count, at):
        zeros = (0,) * len(lead)
        return pl.BlockSpec(lead + (count, wide), lambda i: zeros + (at, i))

    return pl.pallas_call(
        edge_kernel,
        grid=(channels // wide,),
        in_specs=[
            part((3,), 16, 0),
            part((3,), 32, rows // 32 - 1),
            part((2,), 144, 0),
            part((2,), 32, rows // 32 - 1),
            part((), 144, 0),
            part((3,), 3, 0),
            part((3,), 3, 0),
            part((), 7, 0),
        ],
        out_specs=[part((), 32, 0), part((), 176, 0)],
        out_shape=[
            jax.ShapeDtypeStruct((32, channels), BF16),
            jax.ShapeDtypeStruct((176, channels), BF16),
        ],
        scratch_shapes=[
            f32_rows(5, 160),
            f32_rows(32),
            f32_rows(32),
            f32_rows(32),
            f32_rows(32),
        ],
        compiler_params=pltpu.CompilerParams(vmem_limit_bytes=56 * 2**20),
        name="edges",
    )(se, se, mr, mr, g, sw, mw, sf)


def ctx_shares(short_rows, medium_part):
    count = lax.axis_size("ctx")
    depth = medium_part.shape[0] // count
    terms = jnp.concatenate(
        [
            medium_part.reshape(count, depth, -1),
            short_rows.reshape(count, depth, -1),
        ],
        axis=2,
    )
    return lax.all_to_all(terms, "ctx", 0, 0, tiled=True)


def ctx_totals(shares):
    count, depth, width = shares.shape
    channels = width * count * depth // (count * depth + 8)
    total = jnp.sum(shares.astype(F32), axis=0).astype(BF16)
    copies = jnp.broadcast_to(total[None], shares.shape)
    totals = lax.all_to_all(copies, "ctx", 0, 0, tiled=True).astype(F32)
    medium_total = totals[:, :, :channels].reshape(count * depth, channels)
    short_total = totals[:, :, channels:].reshape(8, channels)[:7]
    return short_total, medium_total


def local(tables, se_input, mr_input, g, sw, mw, sf, mf, decay_rate):
    rows, channels = g.shape
    end = rows + REACH
    count = lax.axis_size("ctx")
    norm_factor = 1.0 / math.sqrt(rows * count)
    fwd, rim, inv = (jnp.asarray(table) for table in tables)
    se = jnp.transpose(se_input, (1, 0, 2))
    mr = jnp.transpose(mr_input, (1, 0, 2))
    onward = [(i, i + 1) for i in range(count - 1)]
    backward = [(i, i - 1) for i in range(1, count)]
    rate = decay_rate[None, :]

    last, first = edges(se, mr, g, sw, mw, sf)
    before = lax.ppermute(last, "ctx", onward)
    before, first = lax.optimization_barrier((before, first))
    ahead = lax.ppermute(first, "ctx", backward)
    q1, z1, k2, v2, ps, product, own_d = blocks_call(
        "forward",
        forward_kernel,
        [se, mr, g, before, sw, mw, sf],
        [fwd],
        [
            ((rows,), F32),
            ((rows,), F32),
            ((rows,), F32),
            ((rows,), F32),
            ((rows,), BF16),
            ((rows,), BF16),
            ((POINTS,), F32),
        ],
        [
            f32_rows(5, PAD + rows),
            f32_rows(PAD + rows),
            f32_rows(PAD + rows),
            f32_rows(32),
            bf16_rows(2, rows),
        ],
        4000,
    )
    behind = lax.ppermute(product[rows - 128 :], "ctx", onward)
    medium_part, short_rows, w2, dy1, feats_ahead, v2_ahead, product_ahead = blocks_call(
        "middle",
        functools.partial(middle_kernel, norm_factor),
        [q1, k2, ps, product, own_d, mf, rate, before, last, ahead, sw, mw, sf],
        [fwd, inv],
        [
            ((128,), BF16),
            ((8,), BF16),
            ((end,), F32),
            ((end,), F32),
            ((5, REACH), F32),
            ((REACH,), F32),
            ((REACH,), BF16),
        ],
        [
            f32_rows(5, 32),
            f32_rows(PAD + rows),
            f32_rows(32),
            f32_rows(32),
            bf16_rows(256),
            f32_rows(end + 16),
            f32_rows(end + 16),
        ],
        4000,
    )
    medium_part, behind = lax.optimization_barrier((medium_part, behind))
    shares = ctx_shares(short_rows, medium_part)
    (se_out,) = blocks_call(
        "se_backward",
        se_backward_kernel,
        [q1, z1, feats_ahead, dy1, se, before, sw, sf],
        [],
        [((3, rows), BF16)],
        [
            f32_rows(2, PAD + rows),
            f32_rows(32),
            f32_rows(3, end + 16),
            f32_rows(end + 16),
        ],
        2000,
    )
    shares, se_out, v2 = lax.optimization_barrier((shares, se_out, v2))
    short_total, medium_total = ctx_totals(shares)
    (mr_out,) = blocks_call(
        "mr_backward",
        mr_backward_kernel,
        [v2, v2_ahead, w2, product, mf, rate, behind, product_ahead, g, ahead, mw],
        [fwd, rim, inv],
        [((2, rows), BF16)],
        [
            bf16_rows(256),
            pltpu.VMEM((end, BLOCK), F32),
            f32_rows(32),
            f32_rows(2, end + 16),
        ],
        2000,
    )
    return (
        jnp.transpose(se_out, (1, 0, 2)),
        jnp.transpose(mr_out, (1, 0, 2)),
        short_total,
        medium_total,
    )


def solution(mesh):
    tables = transform_tables()
    placed = (
        P("ctx", None, "ts"),
        P("ctx", None, "ts"),
        P("ctx", "ts"),
        P(None, None, "ts"),
        P(None, None, "ts"),
        P(None, "ts"),
        P(None, "ts"),
        P("ts"),
    )
    return jax.shard_map(
        functools.partial(local, tables),
        mesh=mesh,
        in_specs=placed,
        out_specs=(P("ctx", None, "ts"), P("ctx", None, "ts"), P(None, "ts"), P(None, "ts")),
        check_vma=False,
    )
```

```python
import functools
import math

import jax
import jax.numpy as jnp
import ml_dtypes
import numpy as np
from jax import lax
from jax.experimental import pallas as pl
from jax.experimental.pallas import tpu as pltpu
from jax.sharding import PartitionSpec as P

F32 = jnp.float32
BF16 = jnp.bfloat16
LANES = 128
BLOCK = 256
PAD = 16
LIMIT = 56 * 2**20
REACH = 16
POINTS = 400
HALF = POINTS // 2
DEPTH = 512


def chunks(begin, end, step=32):
    return [(a, min(step, end - a)) for a in range(begin, end, step)]


def split(value):
    high = value.astype(BF16)
    return high, (value - high.astype(F32)).astype(BF16)


def transform_tables():
    frequency = (np.arange(HALF) + 0.5)[:, None]

    def table_at(places):
        angle = 2.0 * np.pi * frequency * places[None, :] / POINTS
        return np.concatenate([np.cos(angle), -np.sin(angle)], axis=0)

    forward = table_at(np.arange(POINTS))
    behind = table_at(np.concatenate([np.arange(-128, 0), np.arange(256, 256 + REACH)]))
    back = forward.T[: 256 + REACH]
    tables = []
    for table, depth in ((forward, DEPTH), (behind, 256), (back, DEPTH)):
        table = np.pad(table, ((0, 0), (0, depth - table.shape[1])))
        high = table.astype(ml_dtypes.bfloat16)
        low = (table - high.astype(np.float64)).astype(ml_dtypes.bfloat16)
        tables.append(np.stack([high, low]))
    return tables


def weighted(ref, lead, row, count, taps, step):
    total = ref[lead + (pl.ds(row, count), slice(None))] * taps[0]
    for j in range(1, len(taps)):
        total = total + ref[lead + (pl.ds(row + step * j, count), slice(None))] * taps[j]
    return total


def rounded(value):
    return value.astype(BF16).astype(F32)


def dot(a, b):
    return jnp.dot(a, b, preferred_element_type=F32)


def wide_dot(table, rows, columns, value):
    high, low = split(value)
    return (
        dot(table[0, rows, columns], high)
        + dot(table[1, rows, columns], high)
        + dot(table[0, rows, columns], low)
    )


def lanes_of(h):
    return slice(h * LANES, (h + 1) * LANES)


def feature_taps(ref, lanes):
    return [[ref[j, p, lanes][None, :] for j in range(3)] for p in range(3)]


def short_taps(ref, lanes):
    return [ref[j, lanes][None, :] for j in range(7)]


def product_of(first, second, conjugate):
    fr, fi = first[:HALF, :], first[HALF:, :]
    sr, si = second[:HALF, :], second[HALF:, :]
    zeros = jnp.zeros((DEPTH - POINTS, BLOCK), F32)
    if conjugate:
        return jnp.concatenate([fr * sr + fi * si, fr * si - fi * sr, zeros], axis=0)
    return jnp.concatenate([fr * sr - fi * si, fr * si + fi * sr, zeros], axis=0)


def last_kernel(se_end, mr_end, sw_ref, sf_ref, last_ref, x, q1, ps, y1, tail):
    for h in range(se_end.shape[2] // LANES):
        lanes = lanes_of(h)
        sw = feature_taps(sw_ref, lanes)
        sf = short_taps(sf_ref, lanes)
        for p in range(3):
            x[p, 0:32, :] = se_end[p, :, lanes].astype(F32)
        for p in range(2):
            x[3 + p, 0:32, :] = mr_end[:, p, lanes].astype(F32)
        k1 = weighted(x, (1,), 8, 24, sw[1], -1)
        v1 = weighted(x, (2,), 8, 24, sw[2], -1)
        ps[8:32, :] = rounded(k1 * v1)
        q1[8:32, :] = weighted(x, (0,), 8, 24, sw[0], -1)
        y1[16:32, :] = rounded(q1[16:32, :] * weighted(ps, (), 16, 16, sf, -1))
        tail[...] = jnp.zeros((32, LANES), F32)
        tail[0:6, :] = ps[26:32, :]
        tail[6:8, :] = y1[30:32, :]
        for p in range(5):
            tail[8 + 2 * p : 10 + 2 * p, :] = x[p, 30:32, :]
        last_ref[:, lanes] = tail[...].astype(BF16)


def first_kernel(se_start, mr_start, g_ref, mw_ref, after_ref, first_ref, x, y1, tail):
    for h in range(g_ref.shape[1] // LANES):
        lanes = lanes_of(h)
        mw = feature_taps(mw_ref, lanes)
        x[3, 0:PAD, :] = jnp.zeros((PAD, LANES), F32)
        for a, n in chunks(0, 144):
            x[3, pl.ds(PAD + a, n), :] = mr_start[pl.ds(a, n), 0, lanes].astype(F32)
        for a, n in chunks(0, 144):
            q2 = weighted(x, (3,), PAD + a, n, mw[0], -1)
            first_ref[pl.ds(a, n), lanes] = (
                g_ref[pl.ds(a, n), lanes].astype(F32) * q2
            ).astype(BF16)
        for p in range(3):
            x[p, 0:16, :] = se_start[p, :, lanes].astype(F32)
        x[4, 0:16, :] = mr_start[0:16, 1, lanes].astype(F32)
        y1[0:16, :] = g_ref[0:16, lanes].astype(F32)
        tail[...] = jnp.zeros((32, LANES), F32)
        tail[0:2, :] = y1[0:2, :]
        tail[2:4, :] = x[3, PAD : PAD + 2, :]
        tail[4:14, :] = x[4, 0:10, :]
        tail[14:22, :] = x[0, 0:8, :]
        tail[22:24, :] = x[1, 0:2, :]
        tail[24:26, :] = x[2, 0:2, :]
        first_ref[144:176, lanes] = tail[...].astype(BF16)


def medium_spectrum(mf_ref, rate_ref, fwd_ref):
    lag = lax.broadcasted_iota(jnp.int32, (128, BLOCK), 0).astype(F32)
    damping = jnp.exp(-rate_ref[...] * lag) * (2.0 / POINTS)
    return damping, wide_dot(fwd_ref, slice(None), slice(0, 128), mf_ref[...] * damping)


def forward_kernel(
    se_ref,
    mr_ref,
    g_ref,
    before_ref,
    sw_ref,
    mw_ref,
    sf_ref,
    fwd_ref,
    q1_ref,
    z1_ref,
    k2_ref,
    v2_ref,
    ps_ref,
    pb,
    edge_ref,
    own_d,
    x,
    ps,
    y1,
    tail,
    db,
):
    rows = se_ref.shape[1]
    for h in range(BLOCK // LANES):
        lanes = lanes_of(h)
        sw = feature_taps(sw_ref, lanes)
        mw = feature_taps(mw_ref, lanes)
        sf = short_taps(sf_ref, lanes)
        tail[...] = before_ref[:, lanes].astype(F32)
        ps[PAD - 6 : PAD, :] = tail[0:6, :]
        y1[PAD - 2 : PAD, :] = tail[6:8, :]
        for p in range(5):
            x[p, PAD - 2 : PAD, :] = tail[8 + 2 * p : 10 + 2 * p, :]
        for t, n in chunks(0, rows):
            for p in range(3):
                x[p, pl.ds(PAD + t, n), :] = se_ref[p, pl.ds(t, n), lanes].astype(F32)
            for p in range(2):
                x[3 + p, pl.ds(PAD + t, n), :] = mr_ref[pl.ds(t, n), p, lanes].astype(F32)
        for t, n in chunks(0, rows):
            r, at = PAD + t, pl.ds(t, n)
            key = weighted(x, (1,), r, n, sw[1], -1)
            value = weighted(x, (2,), r, n, sw[2], -1)
            product = (key * value).astype(BF16)
            ps_ref[at, lanes] = product
            ps[pl.ds(r, n), :] = product.astype(F32)
            query = weighted(x, (0,), r, n, sw[0], -1)
            q1_ref[at, lanes] = query
            mixed = weighted(ps, (), r, n, sf, -1)
            z1_ref[at, lanes] = mixed
            y1[pl.ds(r, n), :] = rounded(query * mixed)
            key = weighted(x, (4,), r, n, mw[1], -1)
            value = weighted(y1, (), r, n, mw[2], -1)
            k2_ref[at, lanes] = key
            v2_ref[at, lanes] = value
            product = (key * value).astype(BF16)
            pb[at, lanes] = product
            if t >= rows - 128:
                edge_ref[pl.ds(t - (rows - 128), n), lanes] = product
            query = weighted(x, (3,), r, n, mw[0], -1)
            high, low = split(g_ref[at, lanes].astype(F32) * query)
            db[0, at, lanes] = high
            db[1, at, lanes] = low
    own = slice(0, 256)
    own_d[...] = (
        dot(fwd_ref[0, :, own], db[0])
        + dot(fwd_ref[1, :, own], db[0])
        + dot(fwd_ref[0, :, own], db[1])
    )


def middle_kernel(
    norm_factor,
    q1_ref,
    k2_ref,
    ps_ref,
    pb,
    own_d,
    mf_ref,
    rate_ref,
    before_ref,
    last_ref,
    ahead_ref,
    sw_ref,
    mw_ref,
    sf_ref,
    fwd_ref,
    inv_ref,
    w2_out,
    dy1_out,
    feats_out,
    v2_out,
    product_out,
    terms,
    x,
    ps,
    y1,
    tail,
    db,
    d,
    dz,
):
    rows = q1_ref.shape[0]
    top = lax.broadcasted_iota(jnp.int32, (REACH, LANES), 0) < 2
    here = pl.ds(PAD, REACH)
    for h in range(BLOCK // LANES):
        lanes = lanes_of(h)
        sw = feature_taps(sw_ref, lanes)
        mw = feature_taps(mw_ref, lanes)
        sf = short_taps(sf_ref, lanes)
        tail[...] = last_ref[:, lanes].astype(F32)
        ps[PAD - 6 : PAD, :] = tail[0:6, :]
        y1[PAD - 2 : PAD, :] = tail[6:8, :]
        for p in range(5):
            x[p, PAD - 2 : PAD, :] = tail[8 + 2 * p : 10 + 2 * p, :]
            x[p, here, :] = jnp.zeros((REACH, LANES), F32)
        tail[...] = ahead_ref[144:176, lanes].astype(F32)
        x[3, PAD : PAD + 2, :] = tail[2:4, :]
        x[4, PAD : PAD + 10, :] = tail[4:14, :]
        x[0, PAD : PAD + 8, :] = tail[14:22, :]
        x[1, PAD : PAD + 2, :] = tail[22:24, :]
        x[2, PAD : PAD + 2, :] = tail[24:26, :]
        query = weighted(x, (0,), PAD, REACH, sw[0], -1)
        key = weighted(x, (1,), PAD, REACH, sw[1], -1)
        value = weighted(x, (2,), PAD, REACH, sw[2], -1)
        feats_out[0, :, lanes] = query
        feats_out[3, :, lanes] = key
        feats_out[4, :, lanes] = value
        ps[here, :] = rounded(key * value)
        mixed = weighted(ps, (), PAD, REACH, sf, -1)
        feats_out[1, :, lanes] = mixed
        y1[here, :] = rounded(query * mixed)
        key = weighted(x, (4,), PAD, REACH, mw[1], -1)
        value = weighted(y1, (), PAD, REACH, mw[2], -1)
        feats_out[2, :, lanes] = key
        v2_out[:, lanes] = value
        product_out[:, lanes] = jnp.where(top, key * value, 0.0).astype(BF16)
        upstream = tail[0:REACH, :] * weighted(x, (3,), PAD, REACH, mw[0], -1)
        upstream = jnp.where(top, upstream, ahead_ref[0:REACH, lanes].astype(F32))
        db[0:REACH, lanes] = upstream.astype(BF16)
        db[REACH : POINTS - 256, lanes] = ahead_ref[REACH : POINTS - 256, lanes]
        db[POINTS - 256 : 256, lanes] = jnp.zeros((DEPTH - POINTS, LANES), BF16)

    beyond = slice(256, DEPTH)
    damping, kernel = medium_spectrum(mf_ref, rate_ref, fwd_ref)
    own = slice(0, 256)
    pp = dot(fwd_ref[0, :, own], pb[...]) + dot(fwd_ref[1, :, own], pb[...])
    dd = own_d[...] + (dot(fwd_ref[0, :, beyond], db[...]) + dot(fwd_ref[1, :, beyond], db[...]))
    spread = wide_dot(inv_ref, slice(None), slice(None), product_of(kernel, dd, True))
    w2_out[...] = spread
    lagged = wide_dot(inv_ref, slice(0, 128), slice(None), product_of(pp, dd, True))
    step = pl.program_id(0)
    lagged = (lagged * (damping * norm_factor)).astype(BF16)
    columns = pl.ds(pl.multiple_of(step * BLOCK, BLOCK), BLOCK)
    terms[:, :, columns] = lagged.reshape(terms.shape[0], terms.shape[1], BLOCK)

    for h in range(BLOCK // LANES):
        lanes = lanes_of(h)
        mw = feature_taps(mw_ref, lanes)
        tail[...] = before_ref[:, lanes].astype(F32)
        ps[PAD - 6 : PAD, :] = tail[0:6, :]
        for t, n in chunks(0, rows):
            at = pl.ds(t, n)
            ps[pl.ds(PAD + t, n), :] = ps_ref[at, lanes].astype(F32)
            d[at, :] = w2_out[at, lanes] * k2_ref[at, lanes]
        last = pl.ds(rows, REACH)
        d[last, :] = w2_out[last, lanes] * feats_out[2, :, lanes]
        d[rows + REACH : rows + REACH + 8, :] = jnp.zeros((8, LANES), F32)
        dy1_out[last, lanes] = weighted(d, (), rows, REACH, mw[2], 1)
        sums = [jnp.zeros((8, LANES), F32) for _ in range(7)]
        for t, n in chunks(0, rows):
            at = pl.ds(t, n)
            grad = weighted(d, (), t, n, mw[2], 1)
            dy1_out[at, lanes] = grad
            grad = grad * q1_ref[at, lanes]
            for j in range(7):
                term = grad * ps[pl.ds(PAD + t - j, n), :]
                sums[j] = sums[j] + jnp.sum(term.reshape(n // 8, 8, LANES), axis=0)
        for j in range(7):
            tail[j : j + 1, :] = jnp.sum(sums[j], axis=0, keepdims=True)
        tail[7:8, :] = jnp.zeros((1, LANES), F32)
        sums = tail[0:8, :] * norm_factor
        sums = jnp.concatenate([sums[:, None, :], jnp.zeros((8, 1, LANES), F32)], axis=1)
        group = pl.ds(pl.multiple_of((step * (BLOCK // LANES) + h) * 8, 8), 8)
        terms[group, :, terms.shape[2] - LANES :] = sums.astype(BF16)


def spans(rows):
    return [(0, t, n) for t, n in chunks(0, rows)] + [(rows, rows, REACH)]


def se_backward_kernel(
    q1_ref, z1_ref, feats_ahead, dy1, se_ref, before_ref, sw_ref, sf_ref, se_out, x, tail, e, dz
):
    rows = q1_ref.shape[0]
    for h in range(BLOCK // LANES):
        lanes = lanes_of(h)
        sw = feature_taps(sw_ref, lanes)
        sf = short_taps(sf_ref, lanes)
        tail[...] = before_ref[:, lanes].astype(F32)
        for p in range(2):
            x[p, PAD - 2 : PAD, :] = tail[10 + 2 * p : 12 + 2 * p, :]
            for t, n in chunks(0, rows):
                x[p, pl.ds(PAD + t, n), :] = se_ref[1 + p, pl.ds(t, n), lanes].astype(F32)
        for base, t, n in spans(rows):
            at, own = pl.ds(t, n), pl.ds(t - base, n)
            grad = dy1[at, lanes]
            query = feats_ahead[0, own, lanes] if base else q1_ref[own, lanes]
            mixed = feats_ahead[1, own, lanes] if base else z1_ref[own, lanes]
            e[0, at, :] = grad * mixed
            dz[at, :] = grad * query
        for base, t, n in spans(rows):
            at, own = pl.ds(t, n), pl.ds(t - base, n)
            grad = weighted(dz, (), t, n, sf, 1)
            if base:
                key, value = feats_ahead[3, own, lanes], feats_ahead[4, own, lanes]
            else:
                key = weighted(x, (0,), PAD + t, n, sw[1], -1)
                value = weighted(x, (1,), PAD + t, n, sw[2], -1)
            e[1, at, :] = grad * value
            e[2, at, :] = grad * key
        for t, n in chunks(0, rows):
            at = pl.ds(t, n)
            for p in range(3):
                se_out[p, at, lanes] = weighted(e, (p,), t, n, sw[p], 1).astype(BF16)


def mr_backward_kernel(
    v2,
    v2_ahead,
    w2,
    own_ref,
    mf_ref,
    rate_ref,
    behind_ref,
    product_ref,
    g_ref,
    ahead_ref,
    mw_ref,
    fwd_ref,
    rim_ref,
    inv_ref,
    mr_out,
    pb,
    z2,
    tail,
    d,
):
    rows = v2.shape[0]
    pb[0:128, :] = behind_ref[...]
    pb[128 : 128 + REACH, :] = product_ref[...]
    pb[128 + REACH : 256, :] = jnp.zeros((128 - REACH, BLOCK), BF16)
    _, kernel = medium_spectrum(mf_ref, rate_ref, fwd_ref)
    own = slice(0, 256)
    pp = (
        dot(fwd_ref[0, :, own], own_ref[...])
        + dot(fwd_ref[1, :, own], own_ref[...])
        + dot(rim_ref[0], pb[...])
        + dot(rim_ref[1], pb[...])
    )
    z2[...] = wide_dot(inv_ref, slice(None), slice(None), product_of(kernel, pp, False))
    for h in range(BLOCK // LANES):
        lanes = lanes_of(h)
        mw = feature_taps(mw_ref, lanes)
        tail[...] = ahead_ref[144:176, lanes].astype(F32)
        tail[2:16, :] = jnp.zeros((14, LANES), F32)
        for base, t, n in spans(rows):
            at, own = pl.ds(t, n), pl.ds(t - base, n)
            value = v2_ahead[own, lanes] if base else v2[own, lanes]
            d[1, at, :] = w2[at, lanes] * value
            upstream = tail[0:REACH, :] if base else g_ref[at, lanes].astype(F32)
            d[0, at, :] = upstream * z2[at, lanes]
        for t, n in chunks(0, rows):
            pair = [weighted(d, (p,), t, n, mw[p], 1)[:, None, :] for p in range(2)]
            mr_out[pl.ds(t, n), :, lanes] = jnp.concatenate(pair, axis=1).astype(BF16)


def rows_of(*dims):
    return pl.BlockSpec(dims + (BLOCK,), lambda i: (0,) * len(dims) + (i,))


def fixed(array):
    return pl.BlockSpec(array.shape, lambda i: (0,) * len(array.shape))


def f32_rows(*dims):
    return pltpu.VMEM(dims + (LANES,), F32)


def bf16_rows(*dims):
    return pltpu.VMEM(dims + (BLOCK,), BF16)


def blocks_call(name, body, arrays, tables, outs, scratch, flops, whole=()):
    channels = arrays[0].shape[-1]
    return pl.pallas_call(
        body,
        grid=(channels // BLOCK,),
        in_specs=[rows_of(*a.shape[:-1]) for a in arrays] + [fixed(t) for t in tables],
        out_specs=[rows_of(*dims) for dims, _ in outs] + [fixed(a) for a in whole],
        out_shape=[jax.ShapeDtypeStruct(dims + (channels,), kind) for dims, kind in outs]
        + list(whole),
        scratch_shapes=scratch,
        compiler_params=pltpu.CompilerParams(vmem_limit_bytes=LIMIT),
        cost_estimate=pl.CostEstimate(
            flops=flops * 256 * channels, bytes_accessed=16 * 256 * channels, transcendentals=0
        ),
        name=name,
    )(*arrays, *tables)


def edge_call(name, body, parts, out_rows, scratch):
    channels = parts[0][0].shape[-1]
    wide = min(channels, 512)

    def part(lead, count, at):
        zeros = (0,) * len(lead)
        return pl.BlockSpec(lead + (count, wide), lambda i: zeros + (at, i))

    def pairs(count, at):
        return pl.BlockSpec((count, 2, wide), lambda i: (at, 0, i))

    return pl.pallas_call(
        body,
        grid=(channels // wide,),
        in_specs=[
            pairs(count, at) if a.ndim == 3 and a.shape[1] == 2 else part(a.shape[:-2], count, at)
            for a, count, at in parts
        ],
        out_specs=part((), out_rows, 0),
        out_shape=jax.ShapeDtypeStruct((out_rows, channels), BF16),
        scratch_shapes=scratch,
        compiler_params=pltpu.CompilerParams(vmem_limit_bytes=LIMIT),
        name=name,
    )(*(a for a, _, _ in parts))


def edges(se, mr, g, sw, mw, sf):
    end = g.shape[0] // 32 - 1
    last = edge_call(
        "last_rows",
        last_kernel,
        [(se, 32, end), (mr, 32, end), (sw, 3, 0), (sf, 7, 0)],
        32,
        [f32_rows(5, 32)] + [f32_rows(32)] * 4,
    )
    first = edge_call(
        "first_rows",
        first_kernel,
        [(se, 16, 0), (mr, 144, 0), (g, 144, 0), (mw, 3, 0), (last, 32, 0)],
        176,
        [f32_rows(5, 160), f32_rows(32), f32_rows(32)],
    )
    return last, first


def ctx_totals(shares):
    count, depth, width = shares.shape
    channels = width - LANES
    total = jnp.sum(shares.astype(F32), axis=0).astype(BF16)
    copies = jnp.broadcast_to(total[None], shares.shape)
    totals = lax.all_to_all(copies, "ctx", 0, 0, tiled=True).reshape(64, 2, width).astype(F32)
    medium_total = totals[:, :, :channels].reshape(count * depth, channels)
    short_total = totals[: channels // 16, 0, channels:].reshape(-1, 8, LANES)
    short_total = jnp.swapaxes(short_total, 0, 1).reshape(8, channels)[:7]
    return short_total, medium_total


def local(tables, se_input, mr_input, g, sw, mw, sf, mf, decay_rate):
    rows, channels = g.shape
    end = rows + REACH
    count = lax.axis_size("ctx")
    norm_factor = 1.0 / math.sqrt(rows * count)
    fwd, rim, inv = (jnp.asarray(table) for table in tables)
    se = jnp.transpose(se_input, (1, 0, 2))
    mr = mr_input
    onward = [(i, i + 1) for i in range(count - 1)]
    backward = [(i, i - 1) for i in range(1, count)]
    rate = decay_rate[None, :]

    last, first = edges(se, mr, g, sw, mw, sf)
    before = lax.ppermute(last, "ctx", onward)
    before, first = lax.optimization_barrier((before, first))
    ahead = lax.ppermute(first, "ctx", backward)
    q1, z1, k2, v2, ps, product, edge, own_d = blocks_call(
        "forward",
        forward_kernel,
        [se, mr, g, before, sw, mw, sf],
        [fwd],
        [
            ((rows,), F32),
            ((rows,), F32),
            ((rows,), F32),
            ((rows,), F32),
            ((rows,), BF16),
            ((rows,), BF16),
            ((128,), BF16),
            ((POINTS,), F32),
        ],
        [
            f32_rows(5, PAD + rows),
            f32_rows(PAD + rows),
            f32_rows(PAD + rows),
            f32_rows(32),
            bf16_rows(2, rows),
        ],
        4000,
    )
    w2, dy1, feats_ahead, v2_ahead, product_ahead, terms = blocks_call(
        "middle",
        functools.partial(middle_kernel, norm_factor),
        [q1, k2, ps, product, own_d, mf, rate, before, last, ahead, sw, mw, sf],
        [fwd, inv],
        [
            ((end,), F32),
            ((end,), F32),
            ((5, REACH), F32),
            ((REACH,), F32),
            ((REACH,), BF16),
        ],
        [
            f32_rows(5, 32),
            f32_rows(PAD + rows),
            f32_rows(32),
            f32_rows(32),
            bf16_rows(256),
            f32_rows(end + 16),
            f32_rows(end + 16),
        ],
        4000,
        [jax.ShapeDtypeStruct((64, 2, channels + LANES), BF16)],
    )
    terms, edge = lax.optimization_barrier((terms, edge))
    behind = lax.ppermute(edge, "ctx", onward)
    terms = terms.reshape(count, 128 // count, channels + LANES)
    shares = lax.all_to_all(terms, "ctx", 0, 0, tiled=True)
    (se_out,) = blocks_call(
        "se_backward",
        se_backward_kernel,
        [q1, z1, feats_ahead, dy1, se, before, sw, sf],
        [],
        [((3, rows), BF16)],
        [
            f32_rows(2, PAD + rows),
            f32_rows(32),
            f32_rows(3, end + 16),
            f32_rows(end + 16),
        ],
        2000,
    )
    shares, se_out, behind = lax.optimization_barrier((shares, se_out, behind))
    short_total, medium_total = ctx_totals(shares)
    (mr_out,) = blocks_call(
        "mr_backward",
        mr_backward_kernel,
        [v2, v2_ahead, w2, product, mf, rate, behind, product_ahead, g, ahead, mw],
        [fwd, rim, inv],
        [((rows, 2), BF16)],
        [
            bf16_rows(256),
            pltpu.VMEM((end, BLOCK), F32),
            f32_rows(32),
            f32_rows(2, end + 16),
        ],
        2000,
    )
    return (
        jnp.transpose(se_out, (1, 0, 2)),
        mr_out,
        short_total,
        medium_total,
    )


def solution(mesh):
    tables = transform_tables()
    placed = (
        P("ctx", None, "ts"),
        P("ctx", None, "ts"),
        P("ctx", "ts"),
        P(None, None, "ts"),
        P(None, None, "ts"),
        P(None, "ts"),
        P(None, "ts"),
        P("ts"),
    )
    return jax.shard_map(
        functools.partial(local, tables),
        mesh=mesh,
        in_specs=placed,
        out_specs=(P("ctx", None, "ts"), P("ctx", None, "ts"), P(None, "ts"), P(None, "ts")),
        check_vma=False,
    )
```

```python
import functools
import math

import jax
import jax.numpy as jnp
import ml_dtypes
import numpy as np
from jax import lax
from jax.experimental import pallas as pl
from jax.experimental.pallas import tpu as pltpu
from jax.sharding import PartitionSpec as P

F32 = jnp.float32
BF16 = jnp.bfloat16
LANES = 128
BLOCK = 256
PAD = 16
LIMIT = 56 * 2**20
REACH = 16
POINTS = 400
HALF = POINTS // 2
DEPTH = 512


def chunks(begin, end, step=32):
    return [(a, min(step, end - a)) for a in range(begin, end, step)]


def split(value):
    high = value.astype(BF16)
    return high, (value - high.astype(F32)).astype(BF16)


def transform_tables():
    frequency = (np.arange(HALF) + 0.5)[:, None]

    def table_at(places):
        angle = 2.0 * np.pi * frequency * places[None, :] / POINTS
        return np.concatenate([np.cos(angle), -np.sin(angle)], axis=0)

    forward = table_at(np.arange(POINTS))
    behind = table_at(np.concatenate([np.arange(-128, 0), np.arange(256, 256 + REACH)]))
    back = forward.T[: 256 + REACH]
    tables = []
    for table, depth in ((forward, DEPTH), (behind, 256), (back, DEPTH)):
        table = np.pad(table, ((0, 0), (0, depth - table.shape[1])))
        high = table.astype(ml_dtypes.bfloat16)
        low = (table - high.astype(np.float64)).astype(ml_dtypes.bfloat16)
        tables.append(np.stack([high, low]))
    return tables


def weighted(ref, lead, row, count, taps, step):
    total = ref[lead + (pl.ds(row, count), slice(None))] * taps[0]
    for j in range(1, len(taps)):
        total = total + ref[lead + (pl.ds(row + step * j, count), slice(None))] * taps[j]
    return total


def rounded(value):
    return value.astype(BF16).astype(F32)


def dot(a, b):
    return jnp.dot(a, b, preferred_element_type=F32)


def wide_dot(table, rows, columns, value):
    high, low = split(value)
    return (
        dot(table[0, rows, columns], high)
        + dot(table[1, rows, columns], high)
        + dot(table[0, rows, columns], low)
    )


def lanes_of(h):
    return slice(h * LANES, (h + 1) * LANES)


def feature_taps(ref, lanes):
    return [[ref[j, p, lanes][None, :] for j in range(3)] for p in range(3)]


def short_taps(ref, lanes):
    return [ref[j, lanes][None, :] for j in range(7)]


def product_of(first, second, conjugate):
    fr, fi = first[:HALF, :], first[HALF:, :]
    sr, si = second[:HALF, :], second[HALF:, :]
    zeros = jnp.zeros((DEPTH - POINTS, BLOCK), F32)
    if conjugate:
        return jnp.concatenate([fr * sr + fi * si, fr * si - fi * sr, zeros], axis=0)
    return jnp.concatenate([fr * sr - fi * si, fr * si + fi * sr, zeros], axis=0)


def last_kernel(se_end, mr_end, sw_ref, sf_ref, last_ref, x, q1, ps, y1, tail):
    for h in range(se_end.shape[2] // LANES):
        lanes = lanes_of(h)
        sw = feature_taps(sw_ref, lanes)
        sf = short_taps(sf_ref, lanes)
        for p in range(3):
            x[p, 0:32, :] = se_end[p, :, lanes].astype(F32)
        for p in range(2):
            x[3 + p, 0:32, :] = mr_end[:, p, lanes].astype(F32)
        k1 = weighted(x, (1,), 8, 24, sw[1], -1)
        v1 = weighted(x, (2,), 8, 24, sw[2], -1)
        ps[8:32, :] = rounded(k1 * v1)
        q1[8:32, :] = weighted(x, (0,), 8, 24, sw[0], -1)
        y1[16:32, :] = rounded(q1[16:32, :] * weighted(ps, (), 16, 16, sf, -1))
        tail[...] = jnp.zeros((32, LANES), F32)
        tail[0:6, :] = ps[26:32, :]
        tail[6:8, :] = y1[30:32, :]
        for p in range(5):
            tail[8 + 2 * p : 10 + 2 * p, :] = x[p, 30:32, :]
        last_ref[:, lanes] = tail[...].astype(BF16)


def first_kernel(se_start, mr_start, g_ref, mw_ref, after_ref, first_ref, x, y1, tail, pairs):
    for h in range(g_ref.shape[1] // LANES):
        lanes = lanes_of(h)
        mw = feature_taps(mw_ref, lanes)
        x[3, 0:PAD, :] = jnp.zeros((PAD, LANES), F32)
        for a, n in chunks(0, 144):
            both = mr_start[pl.ds(a, n), :, lanes].reshape(2 * n, LANES)
            pairs[pl.ds(2 * a, 2 * n), :] = both.astype(F32)
            x[3, pl.ds(PAD + a, n), :] = pairs[pl.ds(2 * a, n, 2), :]
        for a, n in chunks(0, 144):
            q2 = weighted(x, (3,), PAD + a, n, mw[0], -1)
            first_ref[pl.ds(a, n), lanes] = (
                g_ref[pl.ds(a, n), lanes].astype(F32) * q2
            ).astype(BF16)
        for p in range(3):
            x[p, 0:16, :] = se_start[p, :, lanes].astype(F32)
        x[4, 0:16, :] = pairs[pl.ds(1, 16, 2), :]
        y1[0:16, :] = g_ref[0:16, lanes].astype(F32)
        tail[...] = jnp.zeros((32, LANES), F32)
        tail[0:2, :] = y1[0:2, :]
        tail[2:4, :] = x[3, PAD : PAD + 2, :]
        tail[4:14, :] = x[4, 0:10, :]
        tail[14:22, :] = x[0, 0:8, :]
        tail[22:24, :] = x[1, 0:2, :]
        tail[24:26, :] = x[2, 0:2, :]
        first_ref[144:176, lanes] = tail[...].astype(BF16)


def medium_spectrum(mf_ref, rate_ref, fwd_ref):
    lag = lax.broadcasted_iota(jnp.int32, (128, BLOCK), 0).astype(F32)
    damping = jnp.exp(-rate_ref[...] * lag) * (2.0 / POINTS)
    return damping, wide_dot(fwd_ref, slice(None), slice(0, 128), mf_ref[...] * damping)


def forward_kernel(
    se_ref,
    mr_ref,
    g_ref,
    before_ref,
    sw_ref,
    mw_ref,
    sf_ref,
    fwd_ref,
    q1_ref,
    z1_ref,
    k2_ref,
    v2_ref,
    ps_ref,
    pb,
    edge_ref,
    own_d,
    x,
    ps,
    y1,
    tail,
    db,
    pairs,
):
    rows = se_ref.shape[1]
    for h in range(BLOCK // LANES):
        lanes = lanes_of(h)
        sw = feature_taps(sw_ref, lanes)
        mw = feature_taps(mw_ref, lanes)
        sf = short_taps(sf_ref, lanes)
        tail[...] = before_ref[:, lanes].astype(F32)
        ps[PAD - 6 : PAD, :] = tail[0:6, :]
        y1[PAD - 2 : PAD, :] = tail[6:8, :]
        for p in range(5):
            x[p, PAD - 2 : PAD, :] = tail[8 + 2 * p : 10 + 2 * p, :]
        for t, n in chunks(0, rows):
            for p in range(3):
                x[p, pl.ds(PAD + t, n), :] = se_ref[p, pl.ds(t, n), lanes].astype(F32)
            both = mr_ref[pl.ds(t, n), :, lanes].reshape(2 * n, LANES)
            pairs[pl.ds(2 * t, 2 * n), :] = both.astype(F32)
            for p in range(2):
                x[3 + p, pl.ds(PAD + t, n), :] = pairs[pl.ds(2 * t + p, n, 2), :]
        for t, n in chunks(0, rows):
            r, at = PAD + t, pl.ds(t, n)
            key = weighted(x, (1,), r, n, sw[1], -1)
            value = weighted(x, (2,), r, n, sw[2], -1)
            product = (key * value).astype(BF16)
            ps_ref[at, lanes] = product
            ps[pl.ds(r, n), :] = product.astype(F32)
            query = weighted(x, (0,), r, n, sw[0], -1)
            q1_ref[at, lanes] = query
            mixed = weighted(ps, (), r, n, sf, -1)
            z1_ref[at, lanes] = mixed
            y1[pl.ds(r, n), :] = rounded(query * mixed)
            key = weighted(x, (4,), r, n, mw[1], -1)
            value = weighted(y1, (), r, n, mw[2], -1)
            k2_ref[at, lanes] = key
            v2_ref[at, lanes] = value
            product = (key * value).astype(BF16)
            pb[at, lanes] = product
            if t >= rows - 128:
                edge_ref[pl.ds(t - (rows - 128), n), lanes] = product
            query = weighted(x, (3,), r, n, mw[0], -1)
            high, low = split(g_ref[at, lanes].astype(F32) * query)
            db[0, at, lanes] = high
            db[1, at, lanes] = low
    own = slice(0, 256)
    own_d[...] = (
        dot(fwd_ref[0, :, own], db[0])
        + dot(fwd_ref[1, :, own], db[0])
        + dot(fwd_ref[0, :, own], db[1])
    )


def middle_kernel(
    norm_factor,
    q1_ref,
    k2_ref,
    ps_ref,
    pb,
    own_d,
    mf_ref,
    rate_ref,
    before_ref,
    last_ref,
    ahead_ref,
    sw_ref,
    mw_ref,
    sf_ref,
    fwd_ref,
    inv_ref,
    w2_out,
    dy1_out,
    feats_out,
    v2_out,
    product_out,
    terms,
    x,
    ps,
    y1,
    tail,
    db,
    d,
    dz,
):
    rows = q1_ref.shape[0]
    top = lax.broadcasted_iota(jnp.int32, (REACH, LANES), 0) < 2
    here = pl.ds(PAD, REACH)
    for h in range(BLOCK // LANES):
        lanes = lanes_of(h)
        sw = feature_taps(sw_ref, lanes)
        mw = feature_taps(mw_ref, lanes)
        sf = short_taps(sf_ref, lanes)
        tail[...] = last_ref[:, lanes].astype(F32)
        ps[PAD - 6 : PAD, :] = tail[0:6, :]
        y1[PAD - 2 : PAD, :] = tail[6:8, :]
        for p in range(5):
            x[p, PAD - 2 : PAD, :] = tail[8 + 2 * p : 10 + 2 * p, :]
            x[p, here, :] = jnp.zeros((REACH, LANES), F32)
        tail[...] = ahead_ref[144:176, lanes].astype(F32)
        x[3, PAD : PAD + 2, :] = tail[2:4, :]
        x[4, PAD : PAD + 10, :] = tail[4:14, :]
        x[0, PAD : PAD + 8, :] = tail[14:22, :]
        x[1, PAD : PAD + 2, :] = tail[22:24, :]
        x[2, PAD : PAD + 2, :] = tail[24:26, :]
        query = weighted(x, (0,), PAD, REACH, sw[0], -1)
        key = weighted(x, (1,), PAD, REACH, sw[1], -1)
        value = weighted(x, (2,), PAD, REACH, sw[2], -1)
        feats_out[0, :, lanes] = query
        feats_out[3, :, lanes] = key
        feats_out[4, :, lanes] = value
        ps[here, :] = rounded(key * value)
        mixed = weighted(ps, (), PAD, REACH, sf, -1)
        feats_out[1, :, lanes] = mixed
        y1[here, :] = rounded(query * mixed)
        key = weighted(x, (4,), PAD, REACH, mw[1], -1)
        value = weighted(y1, (), PAD, REACH, mw[2], -1)
        feats_out[2, :, lanes] = key
        v2_out[:, lanes] = value
        product_out[:, lanes] = jnp.where(top, key * value, 0.0).astype(BF16)
        upstream = tail[0:REACH, :] * weighted(x, (3,), PAD, REACH, mw[0], -1)
        upstream = jnp.where(top, upstream, ahead_ref[0:REACH, lanes].astype(F32))
        db[0:REACH, lanes] = upstream.astype(BF16)
        db[REACH : POINTS - 256, lanes] = ahead_ref[REACH : POINTS - 256, lanes]
        db[POINTS - 256 : 256, lanes] = jnp.zeros((DEPTH - POINTS, LANES), BF16)

    beyond = slice(256, DEPTH)
    damping, kernel = medium_spectrum(mf_ref, rate_ref, fwd_ref)
    own = slice(0, 256)
    pp = dot(fwd_ref[0, :, own], pb[...]) + dot(fwd_ref[1, :, own], pb[...])
    dd = own_d[...] + (dot(fwd_ref[0, :, beyond], db[...]) + dot(fwd_ref[1, :, beyond], db[...]))
    spread = wide_dot(inv_ref, slice(None), slice(None), product_of(kernel, dd, True))
    w2_out[...] = spread
    lagged = wide_dot(inv_ref, slice(0, 128), slice(None), product_of(pp, dd, True))
    step = pl.program_id(0)
    lagged = (lagged * (damping * norm_factor)).astype(BF16)
    columns = pl.ds(pl.multiple_of(step * BLOCK, BLOCK), BLOCK)
    terms[:, :, columns] = lagged.reshape(terms.shape[0], terms.shape[1], BLOCK)

    for h in range(BLOCK // LANES):
        lanes = lanes_of(h)
        mw = feature_taps(mw_ref, lanes)
        tail[...] = before_ref[:, lanes].astype(F32)
        ps[PAD - 6 : PAD, :] = tail[0:6, :]
        for t, n in chunks(0, rows):
            at = pl.ds(t, n)
            ps[pl.ds(PAD + t, n), :] = ps_ref[at, lanes].astype(F32)
            d[at, :] = w2_out[at, lanes] * k2_ref[at, lanes]
        last = pl.ds(rows, REACH)
        d[last, :] = w2_out[last, lanes] * feats_out[2, :, lanes]
        d[rows + REACH : rows + REACH + 8, :] = jnp.zeros((8, LANES), F32)
        dy1_out[last, lanes] = weighted(d, (), rows, REACH, mw[2], 1)
        sums = [jnp.zeros((8, LANES), F32) for _ in range(7)]
        for t, n in chunks(0, rows):
            at = pl.ds(t, n)
            grad = weighted(d, (), t, n, mw[2], 1)
            dy1_out[at, lanes] = grad
            grad = grad * q1_ref[at, lanes]
            for j in range(7):
                term = grad * ps[pl.ds(PAD + t - j, n), :]
                sums[j] = sums[j] + jnp.sum(term.reshape(n // 8, 8, LANES), axis=0)
        for j in range(7):
            tail[j : j + 1, :] = jnp.sum(sums[j], axis=0, keepdims=True)
        tail[7:8, :] = jnp.zeros((1, LANES), F32)
        sums = tail[0:8, :] * norm_factor
        sums = jnp.concatenate([sums[:, None, :], jnp.zeros((8, 1, LANES), F32)], axis=1)
        group = pl.ds(pl.multiple_of((step * (BLOCK // LANES) + h) * 8, 8), 8)
        terms[group, :, terms.shape[2] - LANES :] = sums.astype(BF16)


def spans(rows):
    return [(0, t, n) for t, n in chunks(0, rows)] + [(rows, rows, REACH)]


def se_backward_kernel(
    q1_ref,
    z1_ref,
    feats_ahead,
    v2,
    v2_ahead,
    w2,
    dy1,
    se_ref,
    before_ref,
    sw_ref,
    mw_ref,
    sf_ref,
    se_out,
    key_out,
    x,
    tail,
    d,
    e,
    dz,
):
    rows = q1_ref.shape[0]
    for h in range(BLOCK // LANES):
        lanes = lanes_of(h)
        sw = feature_taps(sw_ref, lanes)
        sf = short_taps(sf_ref, lanes)
        key_taps = [mw_ref[j, 1, lanes][None, :] for j in range(3)]
        tail[...] = before_ref[:, lanes].astype(F32)
        for p in range(2):
            x[p, PAD - 2 : PAD, :] = tail[10 + 2 * p : 12 + 2 * p, :]
            for t, n in chunks(0, rows):
                x[p, pl.ds(PAD + t, n), :] = se_ref[1 + p, pl.ds(t, n), lanes].astype(F32)
        for base, t, n in spans(rows):
            at, own = pl.ds(t, n), pl.ds(t - base, n)
            value = v2_ahead[own, lanes] if base else v2[own, lanes]
            d[at, :] = w2[at, lanes] * value
            grad = dy1[at, lanes]
            query = feats_ahead[0, own, lanes] if base else q1_ref[own, lanes]
            mixed = feats_ahead[1, own, lanes] if base else z1_ref[own, lanes]
            e[0, at, :] = grad * mixed
            dz[at, :] = grad * query
        for base, t, n in spans(rows):
            at, own = pl.ds(t, n), pl.ds(t - base, n)
            grad = weighted(dz, (), t, n, sf, 1)
            if base:
                key, value = feats_ahead[3, own, lanes], feats_ahead[4, own, lanes]
            else:
                key = weighted(x, (0,), PAD + t, n, sw[1], -1)
                value = weighted(x, (1,), PAD + t, n, sw[2], -1)
            e[1, at, :] = grad * value
            e[2, at, :] = grad * key
        for t, n in chunks(0, rows):
            at = pl.ds(t, n)
            for p in range(3):
                se_out[p, at, lanes] = weighted(e, (p,), t, n, sw[p], 1).astype(BF16)
            key_out[at, lanes] = weighted(d, (), t, n, key_taps, 1).astype(BF16)


def mr_backward_kernel(
    key_grad,
    own_ref,
    mf_ref,
    rate_ref,
    behind_ref,
    product_ref,
    g_ref,
    ahead_ref,
    mw_ref,
    fwd_ref,
    rim_ref,
    inv_ref,
    mr_out,
    pb,
    z2,
    tail,
    d,
    pairs,
):
    rows = key_grad.shape[0]
    pb[0:128, :] = behind_ref[...]
    pb[128 : 128 + REACH, :] = product_ref[...]
    pb[128 + REACH : 256, :] = jnp.zeros((128 - REACH, BLOCK), BF16)
    _, kernel = medium_spectrum(mf_ref, rate_ref, fwd_ref)
    own = slice(0, 256)
    pp = (
        dot(fwd_ref[0, :, own], own_ref[...])
        + dot(fwd_ref[1, :, own], own_ref[...])
        + dot(rim_ref[0], pb[...])
        + dot(rim_ref[1], pb[...])
    )
    z2[...] = wide_dot(inv_ref, slice(None), slice(None), product_of(kernel, pp, False))
    for h in range(BLOCK // LANES):
        lanes = lanes_of(h)
        mw = feature_taps(mw_ref, lanes)
        tail[...] = ahead_ref[144:176, lanes].astype(F32)
        tail[2:16, :] = jnp.zeros((14, LANES), F32)
        for base, t, n in spans(rows):
            at = pl.ds(t, n)
            upstream = tail[0:REACH, :] if base else g_ref[at, lanes].astype(F32)
            d[at, :] = upstream * z2[at, lanes]
        for t, n in chunks(0, rows):
            at = pl.ds(t, n)
            pairs[pl.ds(2 * t, n, 2), :] = weighted(d, (), t, n, mw[0], 1)
            pairs[pl.ds(2 * t + 1, n, 2), :] = key_grad[at, lanes].astype(F32)
            both = pairs[pl.ds(2 * t, 2 * n), :].astype(BF16)
            mr_out[at, :, lanes] = both.reshape(n, 2, LANES)


def rows_of(*dims):
    return pl.BlockSpec(dims + (BLOCK,), lambda i: (0,) * len(dims) + (i,))


def fixed(array):
    return pl.BlockSpec(array.shape, lambda i: (0,) * len(array.shape))


def f32_rows(*dims):
    return pltpu.VMEM(dims + (LANES,), F32)


def bf16_rows(*dims):
    return pltpu.VMEM(dims + (BLOCK,), BF16)


def blocks_call(name, body, arrays, tables, outs, scratch, flops, whole=(), limit=LIMIT):
    channels = arrays[0].shape[-1]
    return pl.pallas_call(
        body,
        grid=(channels // BLOCK,),
        in_specs=[rows_of(*a.shape[:-1]) for a in arrays] + [fixed(t) for t in tables],
        out_specs=[rows_of(*dims) for dims, _ in outs] + [fixed(a) for a in whole],
        out_shape=[jax.ShapeDtypeStruct(dims + (channels,), kind) for dims, kind in outs]
        + list(whole),
        scratch_shapes=scratch,
        compiler_params=pltpu.CompilerParams(vmem_limit_bytes=limit),
        cost_estimate=pl.CostEstimate(
            flops=flops * 256 * channels, bytes_accessed=16 * 256 * channels, transcendentals=0
        ),
        name=name,
    )(*arrays, *tables)


def edge_call(name, body, parts, out_rows, scratch):
    channels = parts[0][0].shape[-1]
    wide = min(channels, 512)

    def part(lead, count, at):
        zeros = (0,) * len(lead)
        return pl.BlockSpec(lead + (count, wide), lambda i: zeros + (at, i))

    def pairs(count, at):
        return pl.BlockSpec((count, 2, wide), lambda i: (at, 0, i))

    return pl.pallas_call(
        body,
        grid=(channels // wide,),
        in_specs=[
            pairs(count, at) if a.ndim == 3 and a.shape[1] == 2 else part(a.shape[:-2], count, at)
            for a, count, at in parts
        ],
        out_specs=part((), out_rows, 0),
        out_shape=jax.ShapeDtypeStruct((out_rows, channels), BF16),
        scratch_shapes=scratch,
        compiler_params=pltpu.CompilerParams(vmem_limit_bytes=LIMIT),
        name=name,
    )(*(a for a, _, _ in parts))


def edges(se, mr, g, sw, mw, sf):
    end = g.shape[0] // 32 - 1
    last = edge_call(
        "last_rows",
        last_kernel,
        [(se, 32, end), (mr, 32, end), (sw, 3, 0), (sf, 7, 0)],
        32,
        [f32_rows(5, 32)] + [f32_rows(32)] * 4,
    )
    first = edge_call(
        "first_rows",
        first_kernel,
        [(se, 16, 0), (mr, 144, 0), (g, 144, 0), (mw, 3, 0), (last, 32, 0)],
        176,
        [f32_rows(5, 160), f32_rows(32), f32_rows(32), f32_rows(288)],
    )
    return last, first


def ctx_totals(shares, behind):
    count, depth, width = shares.shape
    channels = width - LANES
    total = jnp.sum(shares.astype(F32), axis=0).astype(BF16)
    copies = jnp.broadcast_to(total[None], shares.shape)
    copies, behind = lax.optimization_barrier((copies, behind))
    totals = lax.all_to_all(copies, "ctx", 0, 0, tiled=True).reshape(64, 2, width).astype(F32)
    medium_total = totals[:, :, :channels].reshape(count * depth, channels)
    short_total = totals[: channels // 16, 0, channels:].reshape(-1, 8, LANES)
    short_total = jnp.swapaxes(short_total, 0, 1).reshape(8, channels)[:7]
    return short_total, medium_total, behind


def local(tables, se_input, mr_input, g, sw, mw, sf, mf, decay_rate):
    rows, channels = g.shape
    end = rows + REACH
    count = lax.axis_size("ctx")
    norm_factor = 1.0 / math.sqrt(rows * count)
    fwd, rim, inv = (jnp.asarray(table) for table in tables)
    se = jnp.transpose(se_input, (1, 0, 2))
    mr = mr_input
    onward = [(i, i + 1) for i in range(count - 1)]
    backward = [(i, i - 1) for i in range(1, count)]
    rate = decay_rate[None, :]

    last, first = edges(se, mr, g, sw, mw, sf)
    before = lax.ppermute(last, "ctx", onward)
    before, first = lax.optimization_barrier((before, first))
    ahead = lax.ppermute(first, "ctx", backward)
    q1, z1, k2, v2, ps, product, edge, own_d = blocks_call(
        "forward",
        forward_kernel,
        [se, mr, g, before, sw, mw, sf],
        [fwd],
        [
            ((rows,), F32),
            ((rows,), F32),
            ((rows,), F32),
            ((rows,), F32),
            ((rows,), BF16),
            ((rows,), BF16),
            ((128,), BF16),
            ((POINTS,), F32),
        ],
        [
            f32_rows(5, PAD + rows),
            f32_rows(PAD + rows),
            f32_rows(PAD + rows),
            f32_rows(32),
            bf16_rows(2, rows),
            f32_rows(2 * rows),
        ],
        4000,
    )
    w2, dy1, feats_ahead, v2_ahead, product_ahead, terms = blocks_call(
        "middle",
        functools.partial(middle_kernel, norm_factor),
        [q1, k2, ps, product, own_d, mf, rate, before, last, ahead, sw, mw, sf],
        [fwd, inv],
        [
            ((end,), F32),
            ((end,), F32),
            ((5, REACH), F32),
            ((REACH,), F32),
            ((REACH,), BF16),
        ],
        [
            f32_rows(5, 32),
            f32_rows(PAD + rows),
            f32_rows(32),
            f32_rows(32),
            bf16_rows(256),
            f32_rows(end + 16),
            f32_rows(end + 16),
        ],
        4000,
        [jax.ShapeDtypeStruct((64, 2, channels + LANES), BF16)],
    )
    terms, edge = lax.optimization_barrier((terms, edge))
    behind = lax.ppermute(edge, "ctx", onward)
    terms = terms.reshape(count, 128 // count, channels + LANES)
    shares = lax.all_to_all(terms, "ctx", 0, 0, tiled=True)
    se_out, key_grad = blocks_call(
        "se_backward",
        se_backward_kernel,
        [q1, z1, feats_ahead, v2, v2_ahead, w2, dy1, se, before, sw, mw, sf],
        [],
        [((3, rows), BF16), ((rows,), BF16)],
        [
            f32_rows(2, PAD + rows),
            f32_rows(32),
            f32_rows(end + 16),
            f32_rows(3, end + 16),
            f32_rows(end + 16),
        ],
        2000,
    )
    shares, key_grad = lax.optimization_barrier((shares, key_grad))
    short_total, medium_total, behind = ctx_totals(shares, behind)
    (mr_out,) = blocks_call(
        "mr_backward",
        mr_backward_kernel,
        [key_grad, product, mf, rate, behind, product_ahead, g, ahead, mw],
        [fwd, rim, inv],
        [((rows, 2), BF16)],
        [
            bf16_rows(256),
            pltpu.VMEM((end, BLOCK), F32),
            f32_rows(32),
            f32_rows(end + 16),
            f32_rows(2 * rows),
        ],
        2000,
    )
    return (
        jnp.transpose(se_out, (1, 0, 2)),
        mr_out,
        short_total,
        medium_total,
    )


def solution(mesh):
    tables = transform_tables()
    placed = (
        P("ctx", None, "ts"),
        P("ctx", None, "ts"),
        P("ctx", "ts"),
        P(None, None, "ts"),
        P(None, None, "ts"),
        P(None, "ts"),
        P(None, "ts"),
        P("ts"),
    )
    return jax.shard_map(
        functools.partial(local, tables),
        mesh=mesh,
        in_specs=placed,
        out_specs=(P("ctx", None, "ts"), P("ctx", None, "ts"), P(None, "ts"), P(None, "ts")),
        check_vma=False,
    )
```

```python
import functools
import math

import jax
import jax.numpy as jnp
import ml_dtypes
import numpy as np
from jax import lax
from jax.experimental import pallas as pl
from jax.experimental.pallas import tpu as pltpu
from jax.sharding import PartitionSpec as P

F32 = jnp.float32
BF16 = jnp.bfloat16
LANES = 128
BLOCK = 256
PAD = 16
LIMIT = 56 * 2**20
REACH = 16
POINTS = 400
HALF = POINTS // 2
DEPTH = 512


def chunks(begin, end, step=32):
    return [(a, min(step, end - a)) for a in range(begin, end, step)]


def split(value):
    high = value.astype(BF16)
    return high, (value - high.astype(F32)).astype(BF16)


def transform_tables():
    frequency = (np.arange(HALF) + 0.5)[:, None]

    def table_at(places):
        angle = 2.0 * np.pi * frequency * places[None, :] / POINTS
        return np.concatenate([np.cos(angle), -np.sin(angle)], axis=0)

    forward = table_at(np.arange(POINTS))
    behind = table_at(np.concatenate([np.arange(-128, 0), np.arange(256, 256 + REACH)]))
    back = forward.T[: 256 + REACH]
    tables = []
    for table, depth in ((forward, DEPTH), (behind, 256), (back, DEPTH)):
        table = np.pad(table, ((0, 0), (0, depth - table.shape[1])))
        high = table.astype(ml_dtypes.bfloat16)
        low = (table - high.astype(np.float64)).astype(ml_dtypes.bfloat16)
        tables.append(np.stack([high, low]))
    return tables


def weighted(ref, lead, row, count, taps, step):
    total = ref[lead + (pl.ds(row, count), slice(None))] * taps[0]
    for j in range(1, len(taps)):
        total = total + ref[lead + (pl.ds(row + step * j, count), slice(None))] * taps[j]
    return total


def rounded(value):
    return value.astype(BF16).astype(F32)


def dot(a, b):
    return jnp.dot(a, b, preferred_element_type=F32)


def wide_dot(table, rows, columns, value):
    high, low = split(value)
    return (
        dot(table[0, rows, columns], high)
        + dot(table[1, rows, columns], high)
        + dot(table[0, rows, columns], low)
    )


def lanes_of(h):
    return slice(h * LANES, (h + 1) * LANES)


def feature_taps(ref, lanes):
    return [[ref[j, p, lanes][None, :] for j in range(3)] for p in range(3)]


def short_taps(ref, lanes):
    return [ref[j, lanes][None, :] for j in range(7)]


def product_of(first, second, conjugate):
    fr, fi = first[:HALF, :], first[HALF:, :]
    sr, si = second[:HALF, :], second[HALF:, :]
    zeros = jnp.zeros((DEPTH - POINTS, BLOCK), F32)
    if conjugate:
        return jnp.concatenate([fr * sr + fi * si, fr * si - fi * sr, zeros], axis=0)
    return jnp.concatenate([fr * sr - fi * si, fr * si + fi * sr, zeros], axis=0)


def last_kernel(se_end, mr_end, sw_ref, sf_ref, last_ref, x, q1, ps, y1, tail):
    for h in range(se_end.shape[2] // LANES):
        lanes = lanes_of(h)
        sw = feature_taps(sw_ref, lanes)
        sf = short_taps(sf_ref, lanes)
        for p in range(3):
            x[p, 0:32, :] = se_end[p, :, lanes].astype(F32)
        for p in range(2):
            x[3 + p, 0:32, :] = mr_end[:, p, lanes].astype(F32)
        k1 = weighted(x, (1,), 8, 24, sw[1], -1)
        v1 = weighted(x, (2,), 8, 24, sw[2], -1)
        ps[8:32, :] = rounded(k1 * v1)
        q1[8:32, :] = weighted(x, (0,), 8, 24, sw[0], -1)
        y1[16:32, :] = rounded(q1[16:32, :] * weighted(ps, (), 16, 16, sf, -1))
        tail[...] = jnp.zeros((32, LANES), F32)
        tail[0:6, :] = ps[26:32, :]
        tail[6:8, :] = y1[30:32, :]
        for p in range(5):
            tail[8 + 2 * p : 10 + 2 * p, :] = x[p, 30:32, :]
        last_ref[:, lanes] = tail[...].astype(BF16)


def first_kernel(se_start, mr_start, g_ref, mw_ref, after_ref, first_ref, x, y1, tail, pairs):
    for h in range(g_ref.shape[1] // LANES):
        lanes = lanes_of(h)
        mw = feature_taps(mw_ref, lanes)
        x[3, 0:PAD, :] = jnp.zeros((PAD, LANES), F32)
        for a, n in chunks(0, 144):
            both = mr_start[pl.ds(a, n), :, lanes].reshape(2 * n, LANES)
            pairs[pl.ds(2 * a, 2 * n), :] = both.astype(F32)
            x[3, pl.ds(PAD + a, n), :] = pairs[pl.ds(2 * a, n, 2), :]
        for a, n in chunks(0, 144):
            q2 = weighted(x, (3,), PAD + a, n, mw[0], -1)
            first_ref[pl.ds(a, n), lanes] = (
                g_ref[pl.ds(a, n), lanes].astype(F32) * q2
            ).astype(BF16)
        for p in range(3):
            x[p, 0:16, :] = se_start[p, :, lanes].astype(F32)
        x[4, 0:16, :] = pairs[pl.ds(1, 16, 2), :]
        y1[0:16, :] = g_ref[0:16, lanes].astype(F32)
        tail[...] = jnp.zeros((32, LANES), F32)
        tail[0:2, :] = y1[0:2, :]
        tail[2:4, :] = x[3, PAD : PAD + 2, :]
        tail[4:14, :] = x[4, 0:10, :]
        tail[14:22, :] = x[0, 0:8, :]
        tail[22:24, :] = x[1, 0:2, :]
        tail[24:26, :] = x[2, 0:2, :]
        first_ref[144:176, lanes] = tail[...].astype(BF16)


def medium_spectrum(mf_ref, rate_ref, fwd_ref):
    lag = lax.broadcasted_iota(jnp.int32, (128, BLOCK), 0).astype(F32)
    damping = jnp.exp(-rate_ref[...] * lag) * (2.0 / POINTS)
    return damping, wide_dot(fwd_ref, slice(None), slice(0, 128), mf_ref[...] * damping)


def forward_kernel(
    se_ref,
    mr_ref,
    g_ref,
    before_ref,
    sw_ref,
    mw_ref,
    sf_ref,
    fwd_ref,
    q1_ref,
    z1_ref,
    k2_ref,
    v2_ref,
    ps_ref,
    pb,
    edge_ref,
    own_d,
    x,
    ps,
    y1,
    tail,
    db,
    pairs,
):
    rows = se_ref.shape[1]
    for h in range(BLOCK // LANES):
        lanes = lanes_of(h)
        sw = feature_taps(sw_ref, lanes)
        mw = feature_taps(mw_ref, lanes)
        sf = short_taps(sf_ref, lanes)
        tail[...] = before_ref[:, lanes].astype(F32)
        ps[PAD - 6 : PAD, :] = tail[0:6, :]
        y1[PAD - 2 : PAD, :] = tail[6:8, :]
        for p in range(5):
            x[p, PAD - 2 : PAD, :] = tail[8 + 2 * p : 10 + 2 * p, :]
        for t, n in chunks(0, rows):
            for p in range(3):
                x[p, pl.ds(PAD + t, n), :] = se_ref[p, pl.ds(t, n), lanes].astype(F32)
            both = mr_ref[pl.ds(t, n), :, lanes].reshape(2 * n, LANES)
            pairs[pl.ds(2 * t, 2 * n), :] = both.astype(F32)
            for p in range(2):
                x[3 + p, pl.ds(PAD + t, n), :] = pairs[pl.ds(2 * t + p, n, 2), :]
        for t, n in chunks(0, rows):
            r, at = PAD + t, pl.ds(t, n)
            key = weighted(x, (1,), r, n, sw[1], -1)
            value = weighted(x, (2,), r, n, sw[2], -1)
            product = (key * value).astype(BF16)
            ps_ref[at, lanes] = product
            ps[pl.ds(r, n), :] = product.astype(F32)
            query = weighted(x, (0,), r, n, sw[0], -1)
            q1_ref[at, lanes] = query
            mixed = weighted(ps, (), r, n, sf, -1)
            z1_ref[at, lanes] = mixed
            y1[pl.ds(r, n), :] = rounded(query * mixed)
            key = weighted(x, (4,), r, n, mw[1], -1)
            value = weighted(y1, (), r, n, mw[2], -1)
            k2_ref[at, lanes] = key
            v2_ref[at, lanes] = value
            product = (key * value).astype(BF16)
            pb[at, lanes] = product
            if t >= rows - 128:
                edge_ref[pl.ds(t - (rows - 128), n), lanes] = product
            query = weighted(x, (3,), r, n, mw[0], -1)
            high, low = split(g_ref[at, lanes].astype(F32) * query)
            db[0, at, lanes] = high
            db[1, at, lanes] = low
    own = slice(0, 256)
    own_d[...] = (
        dot(fwd_ref[0, :, own], db[0])
        + dot(fwd_ref[1, :, own], db[0])
        + dot(fwd_ref[0, :, own], db[1])
    )


def middle_kernel(
    norm_factor,
    q1_ref,
    k2_ref,
    ps_ref,
    pb,
    own_d,
    mf_ref,
    rate_ref,
    before_ref,
    last_ref,
    ahead_ref,
    sw_ref,
    mw_ref,
    sf_ref,
    fwd_ref,
    inv_ref,
    w2_out,
    dy1_out,
    feats_out,
    v2_out,
    product_out,
    terms,
    x,
    ps,
    y1,
    tail,
    db,
    d,
    dz,
):
    rows = q1_ref.shape[0]
    top = lax.broadcasted_iota(jnp.int32, (REACH, LANES), 0) < 2
    here = pl.ds(PAD, REACH)
    for h in range(BLOCK // LANES):
        lanes = lanes_of(h)
        sw = feature_taps(sw_ref, lanes)
        mw = feature_taps(mw_ref, lanes)
        sf = short_taps(sf_ref, lanes)
        tail[...] = last_ref[:, lanes].astype(F32)
        ps[PAD - 6 : PAD, :] = tail[0:6, :]
        y1[PAD - 2 : PAD, :] = tail[6:8, :]
        for p in range(5):
            x[p, PAD - 2 : PAD, :] = tail[8 + 2 * p : 10 + 2 * p, :]
            x[p, here, :] = jnp.zeros((REACH, LANES), F32)
        tail[...] = ahead_ref[144:176, lanes].astype(F32)
        x[3, PAD : PAD + 2, :] = tail[2:4, :]
        x[4, PAD : PAD + 10, :] = tail[4:14, :]
        x[0, PAD : PAD + 8, :] = tail[14:22, :]
        x[1, PAD : PAD + 2, :] = tail[22:24, :]
        x[2, PAD : PAD + 2, :] = tail[24:26, :]
        query = weighted(x, (0,), PAD, REACH, sw[0], -1)
        key = weighted(x, (1,), PAD, REACH, sw[1], -1)
        value = weighted(x, (2,), PAD, REACH, sw[2], -1)
        feats_out[0, :, lanes] = query
        feats_out[3, :, lanes] = key
        feats_out[4, :, lanes] = value
        ps[here, :] = rounded(key * value)
        mixed = weighted(ps, (), PAD, REACH, sf, -1)
        feats_out[1, :, lanes] = mixed
        y1[here, :] = rounded(query * mixed)
        key = weighted(x, (4,), PAD, REACH, mw[1], -1)
        value = weighted(y1, (), PAD, REACH, mw[2], -1)
        feats_out[2, :, lanes] = key
        v2_out[:, lanes] = value
        product_out[:, lanes] = jnp.where(top, key * value, 0.0).astype(BF16)
        upstream = tail[0:REACH, :] * weighted(x, (3,), PAD, REACH, mw[0], -1)
        upstream = jnp.where(top, upstream, ahead_ref[0:REACH, lanes].astype(F32))
        db[0:REACH, lanes] = upstream.astype(BF16)
        db[REACH : POINTS - 256, lanes] = ahead_ref[REACH : POINTS - 256, lanes]
        db[POINTS - 256 : 256, lanes] = jnp.zeros((DEPTH - POINTS, LANES), BF16)

    beyond = slice(256, DEPTH)
    damping, kernel = medium_spectrum(mf_ref, rate_ref, fwd_ref)
    own = slice(0, 256)
    pp = dot(fwd_ref[0, :, own], pb[...]) + dot(fwd_ref[1, :, own], pb[...])
    dd = own_d[...] + (dot(fwd_ref[0, :, beyond], db[...]) + dot(fwd_ref[1, :, beyond], db[...]))
    spread = wide_dot(inv_ref, slice(None), slice(None), product_of(kernel, dd, True))
    w2_out[...] = spread
    lagged = wide_dot(inv_ref, slice(0, 128), slice(None), product_of(pp, dd, True))
    step = pl.program_id(0)
    lagged = (lagged * (damping * norm_factor)).astype(BF16)
    columns = pl.ds(pl.multiple_of(step * BLOCK, BLOCK), BLOCK)
    terms[:, :, columns] = lagged.reshape(terms.shape[0], terms.shape[1], BLOCK)

    for h in range(BLOCK // LANES):
        lanes = lanes_of(h)
        mw = feature_taps(mw_ref, lanes)
        tail[...] = before_ref[:, lanes].astype(F32)
        ps[PAD - 6 : PAD, :] = tail[0:6, :]
        for t, n in chunks(0, rows):
            at = pl.ds(t, n)
            ps[pl.ds(PAD + t, n), :] = ps_ref[at, lanes].astype(F32)
            d[at, :] = w2_out[at, lanes] * k2_ref[at, lanes]
        last = pl.ds(rows, REACH)
        d[last, :] = w2_out[last, lanes] * feats_out[2, :, lanes]
        d[rows + REACH : rows + REACH + 8, :] = jnp.zeros((8, LANES), F32)
        dy1_out[last, lanes] = weighted(d, (), rows, REACH, mw[2], 1)
        sums = [jnp.zeros((8, LANES), F32) for _ in range(7)]
        for t, n in chunks(0, rows):
            at = pl.ds(t, n)
            grad = weighted(d, (), t, n, mw[2], 1)
            dy1_out[at, lanes] = grad
            grad = grad * q1_ref[at, lanes]
            for j in range(7):
                term = grad * ps[pl.ds(PAD + t - j, n), :]
                sums[j] = sums[j] + jnp.sum(term.reshape(n // 8, 8, LANES), axis=0)
        for j in range(7):
            tail[j : j + 1, :] = jnp.sum(sums[j], axis=0, keepdims=True)
        tail[7:8, :] = jnp.zeros((1, LANES), F32)
        sums = tail[0:8, :] * norm_factor
        sums = jnp.concatenate([sums[:, None, :], jnp.zeros((8, 1, LANES), F32)], axis=1)
        group = pl.ds(pl.multiple_of((step * (BLOCK // LANES) + h) * 8, 8), 8)
        terms[group, :, terms.shape[2] - LANES :] = sums.astype(BF16)


def spans(rows):
    return [(0, t, n) for t, n in chunks(0, rows)] + [(rows, rows, REACH)]


def se_backward_kernel(
    q1_ref,
    z1_ref,
    feats_ahead,
    v2,
    v2_ahead,
    w2,
    dy1,
    se_ref,
    before_ref,
    sw_ref,
    mw_ref,
    sf_ref,
    se_out,
    key_out,
    x,
    tail,
    d,
    e,
    dz,
):
    rows = q1_ref.shape[0]
    for h in range(BLOCK // LANES):
        lanes = lanes_of(h)
        sw = feature_taps(sw_ref, lanes)
        sf = short_taps(sf_ref, lanes)
        key_taps = [mw_ref[j, 1, lanes][None, :] for j in range(3)]
        tail[...] = before_ref[:, lanes].astype(F32)
        for p in range(2):
            x[p, PAD - 2 : PAD, :] = tail[10 + 2 * p : 12 + 2 * p, :]
            for t, n in chunks(0, rows):
                x[p, pl.ds(PAD + t, n), :] = se_ref[1 + p, pl.ds(t, n), lanes].astype(F32)
        for base, t, n in spans(rows):
            at, own = pl.ds(t, n), pl.ds(t - base, n)
            value = v2_ahead[own, lanes] if base else v2[own, lanes]
            d[at, :] = w2[at, lanes] * value
            grad = dy1[at, lanes]
            query = feats_ahead[0, own, lanes] if base else q1_ref[own, lanes]
            mixed = feats_ahead[1, own, lanes] if base else z1_ref[own, lanes]
            e[0, at, :] = grad * mixed
            dz[at, :] = grad * query
        for base, t, n in spans(rows):
            at, own = pl.ds(t, n), pl.ds(t - base, n)
            grad = weighted(dz, (), t, n, sf, 1)
            if base:
                key, value = feats_ahead[3, own, lanes], feats_ahead[4, own, lanes]
            else:
                key = weighted(x, (0,), PAD + t, n, sw[1], -1)
                value = weighted(x, (1,), PAD + t, n, sw[2], -1)
            e[1, at, :] = grad * value
            e[2, at, :] = grad * key
        for t, n in chunks(0, rows):
            at = pl.ds(t, n)
            for p in range(3):
                se_out[p, at, lanes] = weighted(e, (p,), t, n, sw[p], 1).astype(BF16)
            key_out[at, lanes] = weighted(d, (), t, n, key_taps, 1).astype(BF16)


def mr_backward_kernel(
    key_grad,
    own_ref,
    mf_ref,
    rate_ref,
    behind_ref,
    product_ref,
    g_ref,
    ahead_ref,
    mw_ref,
    fwd_ref,
    rim_ref,
    inv_ref,
    mr_out,
    pb,
    z2,
    tail,
    d,
    pairs,
):
    rows = key_grad.shape[0]
    pb[0:128, :] = behind_ref[...]
    pb[128 : 128 + REACH, :] = product_ref[...]
    pb[128 + REACH : 256, :] = jnp.zeros((128 - REACH, BLOCK), BF16)
    _, kernel = medium_spectrum(mf_ref, rate_ref, fwd_ref)
    own = slice(0, 256)
    pp = (
        dot(fwd_ref[0, :, own], own_ref[...])
        + dot(fwd_ref[1, :, own], own_ref[...])
        + dot(rim_ref[0], pb[...])
        + dot(rim_ref[1], pb[...])
    )
    z2[...] = wide_dot(inv_ref, slice(None), slice(None), product_of(kernel, pp, False))
    for h in range(BLOCK // LANES):
        lanes = lanes_of(h)
        mw = feature_taps(mw_ref, lanes)
        tail[...] = ahead_ref[144:176, lanes].astype(F32)
        tail[2:16, :] = jnp.zeros((14, LANES), F32)
        for base, t, n in spans(rows):
            at = pl.ds(t, n)
            upstream = tail[0:REACH, :] if base else g_ref[at, lanes].astype(F32)
            d[at, :] = upstream * z2[at, lanes]
        for t, n in chunks(0, rows):
            at = pl.ds(t, n)
            pairs[pl.ds(2 * t, n, 2), :] = weighted(d, (), t, n, mw[0], 1)
            pairs[pl.ds(2 * t + 1, n, 2), :] = key_grad[at, lanes].astype(F32)
            both = pairs[pl.ds(2 * t, 2 * n), :].astype(BF16)
            mr_out[at, :, lanes] = both.reshape(n, 2, LANES)


def rows_of(*dims):
    return pl.BlockSpec(dims + (BLOCK,), lambda i: (0,) * len(dims) + (i,))


def fixed(array):
    return pl.BlockSpec(array.shape, lambda i: (0,) * len(array.shape))


def f32_rows(*dims):
    return pltpu.VMEM(dims + (LANES,), F32)


def bf16_rows(*dims):
    return pltpu.VMEM(dims + (BLOCK,), BF16)


def blocks_call(name, body, arrays, tables, outs, scratch, flops, whole=(), limit=LIMIT):
    channels = arrays[0].shape[-1]
    return pl.pallas_call(
        body,
        grid=(channels // BLOCK,),
        in_specs=[rows_of(*a.shape[:-1]) for a in arrays] + [fixed(t) for t in tables],
        out_specs=[rows_of(*dims) for dims, _ in outs] + [fixed(a) for a in whole],
        out_shape=[jax.ShapeDtypeStruct(dims + (channels,), kind) for dims, kind in outs]
        + list(whole),
        scratch_shapes=scratch,
        compiler_params=pltpu.CompilerParams(vmem_limit_bytes=limit),
        cost_estimate=pl.CostEstimate(
            flops=flops * 256 * channels, bytes_accessed=16 * 256 * channels, transcendentals=0
        ),
        name=name,
    )(*arrays, *tables)


def edge_call(name, body, parts, out_rows, scratch):
    channels = parts[0][0].shape[-1]
    wide = min(channels, 512)

    def part(lead, count, at):
        zeros = (0,) * len(lead)
        return pl.BlockSpec(lead + (count, wide), lambda i: zeros + (at, i))

    def pairs(count, at):
        return pl.BlockSpec((count, 2, wide), lambda i: (at, 0, i))

    return pl.pallas_call(
        body,
        grid=(channels // wide,),
        in_specs=[
            pairs(count, at) if a.ndim == 3 and a.shape[1] == 2 else part(a.shape[:-2], count, at)
            for a, count, at in parts
        ],
        out_specs=part((), out_rows, 0),
        out_shape=jax.ShapeDtypeStruct((out_rows, channels), BF16),
        scratch_shapes=scratch,
        compiler_params=pltpu.CompilerParams(vmem_limit_bytes=LIMIT),
        name=name,
    )(*(a for a, _, _ in parts))


def edges(se, mr, g, sw, mw, sf):
    end = g.shape[0] // 32 - 1
    last = edge_call(
        "last_rows",
        last_kernel,
        [(se, 32, end), (mr, 32, end), (sw, 3, 0), (sf, 7, 0)],
        32,
        [f32_rows(5, 32)] + [f32_rows(32)] * 4,
    )
    first = edge_call(
        "first_rows",
        first_kernel,
        [(se, 16, 0), (mr, 144, 0), (g, 144, 0), (mw, 3, 0), (last, 32, 0)],
        176,
        [f32_rows(5, 160), f32_rows(32), f32_rows(32), f32_rows(288)],
    )
    return last, first


def ctx_totals(shares, behind):
    count, depth, width = shares.shape
    channels = width - LANES
    total = jnp.sum(shares.astype(F32), axis=0).astype(BF16)
    copies = jnp.broadcast_to(total[None], shares.shape)
    totals = lax.all_to_all(copies, "ctx", 0, 0, tiled=True).reshape(64, 2, width).astype(F32)
    medium_total = totals[:, :, :channels].reshape(count * depth, channels)
    short_total = totals[: channels // 16, 0, channels:].reshape(-1, 8, LANES)
    short_total = jnp.swapaxes(short_total, 0, 1).reshape(8, channels)[:7]
    return short_total, medium_total, behind


def local(tables, se_input, mr_input, g, sw, mw, sf, mf, decay_rate):
    rows, channels = g.shape
    end = rows + REACH
    count = lax.axis_size("ctx")
    norm_factor = 1.0 / math.sqrt(rows * count)
    fwd, rim, inv = (jnp.asarray(table) for table in tables)
    se = jnp.transpose(se_input, (1, 0, 2))
    mr = mr_input
    onward = [(i, i + 1) for i in range(count - 1)]
    backward = [(i, i - 1) for i in range(1, count)]
    rate = decay_rate[None, :]

    last, first = edges(se, mr, g, sw, mw, sf)
    before = lax.ppermute(last, "ctx", onward)
    before, first = lax.optimization_barrier((before, first))
    ahead = lax.ppermute(first, "ctx", backward)
    q1, z1, k2, v2, ps, product, edge, own_d = blocks_call(
        "forward",
        forward_kernel,
        [se, mr, g, before, sw, mw, sf],
        [fwd],
        [
            ((rows,), F32),
            ((rows,), F32),
            ((rows,), F32),
            ((rows,), F32),
            ((rows,), BF16),
            ((rows,), BF16),
            ((128,), BF16),
            ((POINTS,), F32),
        ],
        [
            f32_rows(5, PAD + rows),
            f32_rows(PAD + rows),
            f32_rows(PAD + rows),
            f32_rows(32),
            bf16_rows(2, rows),
            f32_rows(2 * rows),
        ],
        4000,
    )
    w2, dy1, feats_ahead, v2_ahead, product_ahead, terms = blocks_call(
        "middle",
        functools.partial(middle_kernel, norm_factor),
        [q1, k2, ps, product, own_d, mf, rate, before, last, ahead, sw, mw, sf],
        [fwd, inv],
        [
            ((end,), F32),
            ((end,), F32),
            ((5, REACH), F32),
            ((REACH,), F32),
            ((REACH,), BF16),
        ],
        [
            f32_rows(5, 32),
            f32_rows(PAD + rows),
            f32_rows(32),
            f32_rows(32),
            bf16_rows(256),
            f32_rows(end + 16),
            f32_rows(end + 16),
        ],
        4000,
        [jax.ShapeDtypeStruct((64, 2, channels + LANES), BF16)],
    )
    behind = lax.ppermute(edge, "ctx", onward)
    terms, behind = lax.optimization_barrier((terms, behind))
    terms = terms.reshape(count, 128 // count, channels + LANES)
    shares = lax.all_to_all(terms, "ctx", 0, 0, tiled=True)
    se_out, key_grad = blocks_call(
        "se_backward",
        se_backward_kernel,
        [q1, z1, feats_ahead, v2, v2_ahead, w2, dy1, se, before, sw, mw, sf],
        [],
        [((3, rows), BF16), ((rows,), BF16)],
        [
            f32_rows(2, PAD + rows),
            f32_rows(32),
            f32_rows(end + 16),
            f32_rows(3, end + 16),
            f32_rows(end + 16),
        ],
        2000,
    )
    shares, key_grad = lax.optimization_barrier((shares, key_grad))
    short_total, medium_total, behind = ctx_totals(shares, behind)
    (mr_out,) = blocks_call(
        "mr_backward",
        mr_backward_kernel,
        [key_grad, product, mf, rate, behind, product_ahead, g, ahead, mw],
        [fwd, rim, inv],
        [((rows, 2), BF16)],
        [
            bf16_rows(256),
            pltpu.VMEM((end, BLOCK), F32),
            f32_rows(32),
            f32_rows(end + 16),
            f32_rows(2 * rows),
        ],
        2000,
    )
    return (
        jnp.transpose(se_out, (1, 0, 2)),
        mr_out,
        short_total,
        medium_total,
    )


def solution(mesh):
    tables = transform_tables()
    placed = (
        P("ctx", None, "ts"),
        P("ctx", None, "ts"),
        P("ctx", "ts"),
        P(None, None, "ts"),
        P(None, None, "ts"),
        P(None, "ts"),
        P(None, "ts"),
        P("ts"),
    )
    return jax.shard_map(
        functools.partial(local, tables),
        mesh=mesh,
        in_specs=placed,
        out_specs=(P("ctx", None, "ts"), P("ctx", None, "ts"), P(None, "ts"), P(None, "ts")),
        check_vma=False,
    )
```

```python
import functools
import math

import jax
import jax.numpy as jnp
import ml_dtypes
import numpy as np
from jax import lax
from jax.experimental import pallas as pl
from jax.experimental.pallas import tpu as pltpu
from jax.sharding import PartitionSpec as P

F32 = jnp.float32
BF16 = jnp.bfloat16
LANES = 128
BLOCK = 512
PAD = 16
LIMIT = 56 * 2**20
REACH = 16
POINTS = 400
HALF = POINTS // 2
DEPTH = 512


def chunks(begin, end, step=32):
    return [(a, min(step, end - a)) for a in range(begin, end, step)]


def split(value):
    high = value.astype(BF16)
    return high, (value - high.astype(F32)).astype(BF16)


def transform_tables():
    frequency = (np.arange(HALF) + 0.5)[:, None]

    def table_at(places):
        angle = 2.0 * np.pi * frequency * places[None, :] / POINTS
        return np.concatenate([np.cos(angle), -np.sin(angle)], axis=0)

    forward = table_at(np.arange(POINTS))
    behind = table_at(np.concatenate([np.arange(-128, 0), np.arange(256, 256 + REACH)]))
    back = forward.T[: 256 + REACH]
    tables = []
    for table, depth in ((forward, DEPTH), (behind, 256), (back, DEPTH)):
        table = np.pad(table, ((0, 0), (0, depth - table.shape[1])))
        high = table.astype(ml_dtypes.bfloat16)
        low = (table - high.astype(np.float64)).astype(ml_dtypes.bfloat16)
        tables.append(np.stack([high, low]))
    return tables


def weighted(ref, lead, row, count, taps, step):
    total = ref[lead + (pl.ds(row, count), slice(None))] * taps[0]
    for j in range(1, len(taps)):
        total = total + ref[lead + (pl.ds(row + step * j, count), slice(None))] * taps[j]
    return total


def rounded(value):
    return value.astype(BF16).astype(F32)


def dot(a, b):
    return jnp.dot(a, b, preferred_element_type=F32)


def wide_dot(table, rows, columns, value):
    high, low = split(value)
    return (
        dot(table[0, rows, columns], high)
        + dot(table[1, rows, columns], high)
        + dot(table[0, rows, columns], low)
    )


def lanes_of(h):
    return slice(h * LANES, (h + 1) * LANES)


def feature_taps(ref, lanes):
    return [[ref[j, p, lanes][None, :] for j in range(3)] for p in range(3)]


def short_taps(ref, lanes):
    return [ref[j, lanes][None, :] for j in range(7)]


def product_of(first, second, conjugate):
    fr, fi = first[:HALF, :], first[HALF:, :]
    sr, si = second[:HALF, :], second[HALF:, :]
    zeros = jnp.zeros((DEPTH - POINTS, BLOCK), F32)
    if conjugate:
        return jnp.concatenate([fr * sr + fi * si, fr * si - fi * sr, zeros], axis=0)
    return jnp.concatenate([fr * sr - fi * si, fr * si + fi * sr, zeros], axis=0)


def last_kernel(se_end, mr_end, sw_ref, sf_ref, last_ref, x, q1, ps, y1, tail):
    for h in range(se_end.shape[2] // LANES):
        lanes = lanes_of(h)
        sw = feature_taps(sw_ref, lanes)
        sf = short_taps(sf_ref, lanes)
        for p in range(3):
            x[p, 0:32, :] = se_end[p, :, lanes].astype(F32)
        for p in range(2):
            x[3 + p, 0:32, :] = mr_end[:, p, lanes].astype(F32)
        k1 = weighted(x, (1,), 8, 24, sw[1], -1)
        v1 = weighted(x, (2,), 8, 24, sw[2], -1)
        ps[8:32, :] = rounded(k1 * v1)
        q1[8:32, :] = weighted(x, (0,), 8, 24, sw[0], -1)
        y1[16:32, :] = rounded(q1[16:32, :] * weighted(ps, (), 16, 16, sf, -1))
        tail[...] = jnp.zeros((32, LANES), F32)
        tail[0:6, :] = ps[26:32, :]
        tail[6:8, :] = y1[30:32, :]
        for p in range(5):
            tail[8 + 2 * p : 10 + 2 * p, :] = x[p, 30:32, :]
        last_ref[:, lanes] = tail[...].astype(BF16)


def first_kernel(se_start, mr_start, g_ref, mw_ref, after_ref, first_ref, x, y1, tail, pairs):
    for h in range(g_ref.shape[1] // LANES):
        lanes = lanes_of(h)
        mw = feature_taps(mw_ref, lanes)
        x[3, 0:PAD, :] = jnp.zeros((PAD, LANES), F32)
        for a, n in chunks(0, 144):
            both = mr_start[pl.ds(a, n), :, lanes].reshape(2 * n, LANES)
            pairs[pl.ds(2 * a, 2 * n), :] = both.astype(F32)
            x[3, pl.ds(PAD + a, n), :] = pairs[pl.ds(2 * a, n, 2), :]
        for a, n in chunks(0, 144):
            q2 = weighted(x, (3,), PAD + a, n, mw[0], -1)
            first_ref[pl.ds(a, n), lanes] = (
                g_ref[pl.ds(a, n), lanes].astype(F32) * q2
            ).astype(BF16)
        for p in range(3):
            x[p, 0:16, :] = se_start[p, :, lanes].astype(F32)
        x[4, 0:16, :] = pairs[pl.ds(1, 16, 2), :]
        y1[0:16, :] = g_ref[0:16, lanes].astype(F32)
        tail[...] = jnp.zeros((32, LANES), F32)
        tail[0:2, :] = y1[0:2, :]
        tail[2:4, :] = x[3, PAD : PAD + 2, :]
        tail[4:14, :] = x[4, 0:10, :]
        tail[14:22, :] = x[0, 0:8, :]
        tail[22:24, :] = x[1, 0:2, :]
        tail[24:26, :] = x[2, 0:2, :]
        first_ref[144:176, lanes] = tail[...].astype(BF16)


def medium_spectrum(mf_ref, rate_ref, fwd_ref):
    lag = lax.broadcasted_iota(jnp.int32, (128, BLOCK), 0).astype(F32)
    damping = jnp.exp(-rate_ref[...] * lag) * (2.0 / POINTS)
    return damping, wide_dot(fwd_ref, slice(None), slice(0, 128), mf_ref[...] * damping)


def forward_kernel(
    se_ref,
    mr_ref,
    g_ref,
    before_ref,
    sw_ref,
    mw_ref,
    sf_ref,
    fwd_ref,
    q1_ref,
    z1_ref,
    k2_ref,
    v2_ref,
    ps_ref,
    pb,
    edge_ref,
    own_d,
    x,
    ps,
    y1,
    tail,
    db,
    pairs,
):
    rows = se_ref.shape[1]
    for h in range(BLOCK // LANES):
        lanes = lanes_of(h)
        sw = feature_taps(sw_ref, lanes)
        mw = feature_taps(mw_ref, lanes)
        sf = short_taps(sf_ref, lanes)
        tail[...] = before_ref[:, lanes].astype(F32)
        ps[PAD - 6 : PAD, :] = tail[0:6, :]
        y1[PAD - 2 : PAD, :] = tail[6:8, :]
        for p in range(5):
            x[p, PAD - 2 : PAD, :] = tail[8 + 2 * p : 10 + 2 * p, :]
        for t, n in chunks(0, rows):
            for p in range(3):
                x[p, pl.ds(PAD + t, n), :] = se_ref[p, pl.ds(t, n), lanes].astype(F32)
            both = mr_ref[pl.ds(t, n), :, lanes].reshape(2 * n, LANES)
            pairs[pl.ds(2 * t, 2 * n), :] = both.astype(F32)
            for p in range(2):
                x[3 + p, pl.ds(PAD + t, n), :] = pairs[pl.ds(2 * t + p, n, 2), :]
        for t, n in chunks(0, rows):
            r, at = PAD + t, pl.ds(t, n)
            key = weighted(x, (1,), r, n, sw[1], -1)
            value = weighted(x, (2,), r, n, sw[2], -1)
            product = (key * value).astype(BF16)
            ps_ref[at, lanes] = product
            ps[pl.ds(r, n), :] = product.astype(F32)
            query = weighted(x, (0,), r, n, sw[0], -1)
            q1_ref[at, lanes] = query
            mixed = weighted(ps, (), r, n, sf, -1)
            z1_ref[at, lanes] = mixed
            y1[pl.ds(r, n), :] = rounded(query * mixed)
            key = weighted(x, (4,), r, n, mw[1], -1)
            value = weighted(y1, (), r, n, mw[2], -1)
            k2_ref[at, lanes] = key
            v2_ref[at, lanes] = value
            product = (key * value).astype(BF16)
            pb[at, lanes] = product
            if t >= rows - 128:
                edge_ref[pl.ds(t - (rows - 128), n), lanes] = product
            query = weighted(x, (3,), r, n, mw[0], -1)
            high, low = split(g_ref[at, lanes].astype(F32) * query)
            db[0, at, lanes] = high
            db[1, at, lanes] = low
    own = slice(0, 256)
    own_d[...] = (
        dot(fwd_ref[0, :, own], db[0])
        + dot(fwd_ref[1, :, own], db[0])
        + dot(fwd_ref[0, :, own], db[1])
    )


def middle_kernel(
    norm_factor,
    q1_ref,
    k2_ref,
    ps_ref,
    pb,
    own_d,
    mf_ref,
    rate_ref,
    before_ref,
    last_ref,
    ahead_ref,
    sw_ref,
    mw_ref,
    sf_ref,
    fwd_ref,
    inv_ref,
    w2_out,
    dy1_out,
    feats_out,
    v2_out,
    product_out,
    terms,
    x,
    ps,
    y1,
    tail,
    db,
    d,
    dz,
):
    rows = q1_ref.shape[0]
    top = lax.broadcasted_iota(jnp.int32, (REACH, LANES), 0) < 2
    here = pl.ds(PAD, REACH)
    for h in range(BLOCK // LANES):
        lanes = lanes_of(h)
        sw = feature_taps(sw_ref, lanes)
        mw = feature_taps(mw_ref, lanes)
        sf = short_taps(sf_ref, lanes)
        tail[...] = last_ref[:, lanes].astype(F32)
        ps[PAD - 6 : PAD, :] = tail[0:6, :]
        y1[PAD - 2 : PAD, :] = tail[6:8, :]
        for p in range(5):
            x[p, PAD - 2 : PAD, :] = tail[8 + 2 * p : 10 + 2 * p, :]
            x[p, here, :] = jnp.zeros((REACH, LANES), F32)
        tail[...] = ahead_ref[144:176, lanes].astype(F32)
        x[3, PAD : PAD + 2, :] = tail[2:4, :]
        x[4, PAD : PAD + 10, :] = tail[4:14, :]
        x[0, PAD : PAD + 8, :] = tail[14:22, :]
        x[1, PAD : PAD + 2, :] = tail[22:24, :]
        x[2, PAD : PAD + 2, :] = tail[24:26, :]
        query = weighted(x, (0,), PAD, REACH, sw[0], -1)
        key = weighted(x, (1,), PAD, REACH, sw[1], -1)
        value = weighted(x, (2,), PAD, REACH, sw[2], -1)
        feats_out[0, :, lanes] = query
        feats_out[3, :, lanes] = key
        feats_out[4, :, lanes] = value
        ps[here, :] = rounded(key * value)
        mixed = weighted(ps, (), PAD, REACH, sf, -1)
        feats_out[1, :, lanes] = mixed
        y1[here, :] = rounded(query * mixed)
        key = weighted(x, (4,), PAD, REACH, mw[1], -1)
        value = weighted(y1, (), PAD, REACH, mw[2], -1)
        feats_out[2, :, lanes] = key
        v2_out[:, lanes] = value
        product_out[:, lanes] = jnp.where(top, key * value, 0.0).astype(BF16)
        upstream = tail[0:REACH, :] * weighted(x, (3,), PAD, REACH, mw[0], -1)
        upstream = jnp.where(top, upstream, ahead_ref[0:REACH, lanes].astype(F32))
        db[0:REACH, lanes] = upstream.astype(BF16)
        db[REACH : POINTS - 256, lanes] = ahead_ref[REACH : POINTS - 256, lanes]
        db[POINTS - 256 : 256, lanes] = jnp.zeros((DEPTH - POINTS, LANES), BF16)

    beyond = slice(256, DEPTH)
    damping, kernel = medium_spectrum(mf_ref, rate_ref, fwd_ref)
    own = slice(0, 256)
    pp = dot(fwd_ref[0, :, own], pb[...]) + dot(fwd_ref[1, :, own], pb[...])
    dd = own_d[...] + (dot(fwd_ref[0, :, beyond], db[...]) + dot(fwd_ref[1, :, beyond], db[...]))
    spread = wide_dot(inv_ref, slice(None), slice(None), product_of(kernel, dd, True))
    w2_out[...] = spread
    lagged = wide_dot(inv_ref, slice(0, 128), slice(None), product_of(pp, dd, True))
    step = pl.program_id(0)
    lagged = (lagged * (damping * norm_factor)).astype(BF16)
    columns = pl.ds(pl.multiple_of(step * BLOCK, BLOCK), BLOCK)
    terms[:, :, columns] = lagged.reshape(terms.shape[0], terms.shape[1], BLOCK)

    for h in range(BLOCK // LANES):
        lanes = lanes_of(h)
        mw = feature_taps(mw_ref, lanes)
        tail[...] = before_ref[:, lanes].astype(F32)
        ps[PAD - 6 : PAD, :] = tail[0:6, :]
        for t, n in chunks(0, rows):
            at = pl.ds(t, n)
            ps[pl.ds(PAD + t, n), :] = ps_ref[at, lanes].astype(F32)
            d[at, :] = w2_out[at, lanes] * k2_ref[at, lanes]
        last = pl.ds(rows, REACH)
        d[last, :] = w2_out[last, lanes] * feats_out[2, :, lanes]
        d[rows + REACH : rows + REACH + 8, :] = jnp.zeros((8, LANES), F32)
        dy1_out[last, lanes] = weighted(d, (), rows, REACH, mw[2], 1)
        sums = [jnp.zeros((8, LANES), F32) for _ in range(7)]
        for t, n in chunks(0, rows):
            at = pl.ds(t, n)
            grad = weighted(d, (), t, n, mw[2], 1)
            dy1_out[at, lanes] = grad
            grad = grad * q1_ref[at, lanes]
            for j in range(7):
                term = grad * ps[pl.ds(PAD + t - j, n), :]
                sums[j] = sums[j] + jnp.sum(term.reshape(n // 8, 8, LANES), axis=0)
        for j in range(7):
            tail[j : j + 1, :] = jnp.sum(sums[j], axis=0, keepdims=True)
        tail[7:8, :] = jnp.zeros((1, LANES), F32)
        sums = tail[0:8, :] * norm_factor
        sums = jnp.concatenate([sums[:, None, :], jnp.zeros((8, 1, LANES), F32)], axis=1)
        group = pl.ds(pl.multiple_of((step * (BLOCK // LANES) + h) * 8, 8), 8)
        terms[group, :, terms.shape[2] - LANES :] = sums.astype(BF16)


def spans(rows):
    return [(0, t, n) for t, n in chunks(0, rows)] + [(rows, rows, REACH)]


def se_backward_kernel(
    q1_ref,
    z1_ref,
    feats_ahead,
    v2,
    v2_ahead,
    w2,
    dy1,
    se_ref,
    before_ref,
    sw_ref,
    mw_ref,
    sf_ref,
    se_out,
    key_out,
    x,
    tail,
    d,
    e,
    dz,
):
    rows = q1_ref.shape[0]
    for h in range(BLOCK // LANES):
        lanes = lanes_of(h)
        sw = feature_taps(sw_ref, lanes)
        sf = short_taps(sf_ref, lanes)
        key_taps = [mw_ref[j, 1, lanes][None, :] for j in range(3)]
        tail[...] = before_ref[:, lanes].astype(F32)
        for p in range(2):
            x[p, PAD - 2 : PAD, :] = tail[10 + 2 * p : 12 + 2 * p, :]
            for t, n in chunks(0, rows):
                x[p, pl.ds(PAD + t, n), :] = se_ref[1 + p, pl.ds(t, n), lanes].astype(F32)
        for base, t, n in spans(rows):
            at, own = pl.ds(t, n), pl.ds(t - base, n)
            value = v2_ahead[own, lanes] if base else v2[own, lanes]
            d[at, :] = w2[at, lanes] * value
            grad = dy1[at, lanes]
            query = feats_ahead[0, own, lanes] if base else q1_ref[own, lanes]
            mixed = feats_ahead[1, own, lanes] if base else z1_ref[own, lanes]
            e[0, at, :] = grad * mixed
            dz[at, :] = grad * query
        for base, t, n in spans(rows):
            at, own = pl.ds(t, n), pl.ds(t - base, n)
            grad = weighted(dz, (), t, n, sf, 1)
            if base:
                key, value = feats_ahead[3, own, lanes], feats_ahead[4, own, lanes]
            else:
                key = weighted(x, (0,), PAD + t, n, sw[1], -1)
                value = weighted(x, (1,), PAD + t, n, sw[2], -1)
            e[1, at, :] = grad * value
            e[2, at, :] = grad * key
        for t, n in chunks(0, rows):
            at = pl.ds(t, n)
            for p in range(3):
                se_out[p, at, lanes] = weighted(e, (p,), t, n, sw[p], 1).astype(BF16)
            key_out[at, lanes] = weighted(d, (), t, n, key_taps, 1).astype(BF16)


def mr_backward_kernel(
    key_grad,
    own_ref,
    mf_ref,
    rate_ref,
    behind_ref,
    product_ref,
    g_ref,
    ahead_ref,
    mw_ref,
    fwd_ref,
    rim_ref,
    inv_ref,
    mr_out,
    pb,
    z2,
    tail,
    d,
    pairs,
):
    rows = key_grad.shape[0]
    pb[0:128, :] = behind_ref[...]
    pb[128 : 128 + REACH, :] = product_ref[...]
    pb[128 + REACH : 256, :] = jnp.zeros((128 - REACH, BLOCK), BF16)
    _, kernel = medium_spectrum(mf_ref, rate_ref, fwd_ref)
    own = slice(0, 256)
    pp = (
        dot(fwd_ref[0, :, own], own_ref[...])
        + dot(fwd_ref[1, :, own], own_ref[...])
        + dot(rim_ref[0], pb[...])
        + dot(rim_ref[1], pb[...])
    )
    z2[...] = wide_dot(inv_ref, slice(None), slice(None), product_of(kernel, pp, False))
    for h in range(BLOCK // LANES):
        lanes = lanes_of(h)
        mw = feature_taps(mw_ref, lanes)
        tail[...] = ahead_ref[144:176, lanes].astype(F32)
        tail[2:16, :] = jnp.zeros((14, LANES), F32)
        for base, t, n in spans(rows):
            at = pl.ds(t, n)
            upstream = tail[0:REACH, :] if base else g_ref[at, lanes].astype(F32)
            d[at, :] = upstream * z2[at, lanes]
        for t, n in chunks(0, rows):
            at = pl.ds(t, n)
            pairs[pl.ds(2 * t, n, 2), :] = weighted(d, (), t, n, mw[0], 1)
            pairs[pl.ds(2 * t + 1, n, 2), :] = key_grad[at, lanes].astype(F32)
            both = pairs[pl.ds(2 * t, 2 * n), :].astype(BF16)
            mr_out[at, :, lanes] = both.reshape(n, 2, LANES)


def rows_of(*dims):
    return pl.BlockSpec(dims + (BLOCK,), lambda i: (0,) * len(dims) + (i,))


def fixed(array):
    return pl.BlockSpec(array.shape, lambda i: (0,) * len(array.shape))


def f32_rows(*dims):
    return pltpu.VMEM(dims + (LANES,), F32)


def bf16_rows(*dims):
    return pltpu.VMEM(dims + (BLOCK,), BF16)


def blocks_call(name, body, arrays, tables, outs, scratch, flops, whole=(), limit=LIMIT):
    channels = arrays[0].shape[-1]
    return pl.pallas_call(
        body,
        grid=(channels // BLOCK,),
        in_specs=[rows_of(*a.shape[:-1]) for a in arrays] + [fixed(t) for t in tables],
        out_specs=[rows_of(*dims) for dims, _ in outs] + [fixed(a) for a in whole],
        out_shape=[jax.ShapeDtypeStruct(dims + (channels,), kind) for dims, kind in outs]
        + list(whole),
        scratch_shapes=scratch,
        compiler_params=pltpu.CompilerParams(vmem_limit_bytes=limit),
        cost_estimate=pl.CostEstimate(
            flops=flops * 256 * channels, bytes_accessed=16 * 256 * channels, transcendentals=0
        ),
        name=name,
    )(*arrays, *tables)


def edge_call(name, body, parts, out_rows, scratch):
    channels = parts[0][0].shape[-1]
    wide = min(channels, 512)

    def part(lead, count, at):
        zeros = (0,) * len(lead)
        return pl.BlockSpec(lead + (count, wide), lambda i: zeros + (at, i))

    def pairs(count, at):
        return pl.BlockSpec((count, 2, wide), lambda i: (at, 0, i))

    return pl.pallas_call(
        body,
        grid=(channels // wide,),
        in_specs=[
            pairs(count, at) if a.ndim == 3 and a.shape[1] == 2 else part(a.shape[:-2], count, at)
            for a, count, at in parts
        ],
        out_specs=part((), out_rows, 0),
        out_shape=jax.ShapeDtypeStruct((out_rows, channels), BF16),
        scratch_shapes=scratch,
        compiler_params=pltpu.CompilerParams(vmem_limit_bytes=LIMIT),
        name=name,
    )(*(a for a, _, _ in parts))


def edges(se, mr, g, sw, mw, sf):
    end = g.shape[0] // 32 - 1
    last = edge_call(
        "last_rows",
        last_kernel,
        [(se, 32, end), (mr, 32, end), (sw, 3, 0), (sf, 7, 0)],
        32,
        [f32_rows(5, 32)] + [f32_rows(32)] * 4,
    )
    first = edge_call(
        "first_rows",
        first_kernel,
        [(se, 16, 0), (mr, 144, 0), (g, 144, 0), (mw, 3, 0), (last, 32, 0)],
        176,
        [f32_rows(5, 160), f32_rows(32), f32_rows(32), f32_rows(288)],
    )
    return last, first


def ctx_totals(shares, behind):
    count, depth, width = shares.shape
    channels = width - LANES
    total = jnp.sum(shares.astype(F32), axis=0).astype(BF16)
    copies = jnp.broadcast_to(total[None], shares.shape)
    totals = lax.all_to_all(copies, "ctx", 0, 0, tiled=True).reshape(64, 2, width).astype(F32)
    medium_total = totals[:, :, :channels].reshape(count * depth, channels)
    short_total = totals[: channels // 16, 0, channels:].reshape(-1, 8, LANES)
    short_total = jnp.swapaxes(short_total, 0, 1).reshape(8, channels)[:7]
    return short_total, medium_total, behind


def local(tables, se_input, mr_input, g, sw, mw, sf, mf, decay_rate):
    rows, channels = g.shape
    end = rows + REACH
    count = lax.axis_size("ctx")
    norm_factor = 1.0 / math.sqrt(rows * count)
    fwd, rim, inv = (jnp.asarray(table) for table in tables)
    se = jnp.transpose(se_input, (1, 0, 2))
    mr = mr_input
    onward = [(i, i + 1) for i in range(count - 1)]
    backward = [(i, i - 1) for i in range(1, count)]
    rate = decay_rate[None, :]

    last, first = edges(se, mr, g, sw, mw, sf)
    before = lax.ppermute(last, "ctx", onward)
    before, first = lax.optimization_barrier((before, first))
    ahead = lax.ppermute(first, "ctx", backward)
    q1, z1, k2, v2, ps, product, edge, own_d = blocks_call(
        "forward",
        forward_kernel,
        [se, mr, g, before, sw, mw, sf],
        [fwd],
        [
            ((rows,), F32),
            ((rows,), F32),
            ((rows,), F32),
            ((rows,), F32),
            ((rows,), BF16),
            ((rows,), BF16),
            ((128,), BF16),
            ((POINTS,), F32),
        ],
        [
            f32_rows(5, PAD + rows),
            f32_rows(PAD + rows),
            f32_rows(PAD + rows),
            f32_rows(32),
            bf16_rows(2, rows),
            f32_rows(2 * rows),
        ],
        4000,
    )
    w2, dy1, feats_ahead, v2_ahead, product_ahead, terms = blocks_call(
        "middle",
        functools.partial(middle_kernel, norm_factor),
        [q1, k2, ps, product, own_d, mf, rate, before, last, ahead, sw, mw, sf],
        [fwd, inv],
        [
            ((end,), F32),
            ((end,), F32),
            ((5, REACH), F32),
            ((REACH,), F32),
            ((REACH,), BF16),
        ],
        [
            f32_rows(5, 32),
            f32_rows(PAD + rows),
            f32_rows(32),
            f32_rows(32),
            bf16_rows(256),
            f32_rows(end + 16),
            f32_rows(end + 16),
        ],
        4000,
        [jax.ShapeDtypeStruct((64, 2, channels + LANES), BF16)],
    )
    behind = lax.ppermute(edge, "ctx", onward)
    terms, behind = lax.optimization_barrier((terms, behind))
    terms = terms.reshape(count, 128 // count, channels + LANES)
    shares = lax.all_to_all(terms, "ctx", 0, 0, tiled=True)
    se_out, key_grad = blocks_call(
        "se_backward",
        se_backward_kernel,
        [q1, z1, feats_ahead, v2, v2_ahead, w2, dy1, se, before, sw, mw, sf],
        [],
        [((3, rows), BF16), ((rows,), BF16)],
        [
            f32_rows(2, PAD + rows),
            f32_rows(32),
            f32_rows(end + 16),
            f32_rows(3, end + 16),
            f32_rows(end + 16),
        ],
        2000,
    )
    shares, key_grad = lax.optimization_barrier((shares, key_grad))
    short_total, medium_total, behind = ctx_totals(shares, behind)
    (mr_out,) = blocks_call(
        "mr_backward",
        mr_backward_kernel,
        [key_grad, product, mf, rate, behind, product_ahead, g, ahead, mw],
        [fwd, rim, inv],
        [((rows, 2), BF16)],
        [
            bf16_rows(256),
            pltpu.VMEM((end, BLOCK), F32),
            f32_rows(32),
            f32_rows(end + 16),
            f32_rows(2 * rows),
        ],
        2000,
    )
    return (
        jnp.transpose(se_out, (1, 0, 2)),
        mr_out,
        short_total,
        medium_total,
    )


def solution(mesh):
    tables = transform_tables()
    placed = (
        P("ctx", None, "ts"),
        P("ctx", None, "ts"),
        P("ctx", "ts"),
        P(None, None, "ts"),
        P(None, None, "ts"),
        P(None, "ts"),
        P(None, "ts"),
        P("ts"),
    )
    return jax.shard_map(
        functools.partial(local, tables),
        mesh=mesh,
        in_specs=placed,
        out_specs=(P("ctx", None, "ts"), P("ctx", None, "ts"), P(None, "ts"), P(None, "ts")),
        check_vma=False,
    )
```
